32 devices in a mesh: group: 2 (over x), chan: 16 (over z, y, core).
Axes of the slice: x: 2, y: 2, z: 4, core: 2. Of those that a mesh axis runs over, the one named last changes fastest.
Arguments:
- voltages: bfloat16 [32, 2, 256, 1024], P(('group', 'chan')), parts along dimension 0, may hold values from -6 to 6
- cal_num: float32 [32, 4, 512], P(('group', 'chan')), parts along dimension 0, may hold values from -6 to 6
- cal_weight: float32 [32, 2, 512], P(('group', 'chan')), parts along dimension 0, may hold values from 0.2 to 5
- flags: int32 [32, 512], P(('group', 'chan')), parts along dimension 0, may hold values 0 or 1
- positions: float32 [2, 512], replicated, may hold values from -300 to 300
- directions: float32 [2, 1024], replicated, may hold values from -0.05 to 0.05
- pointing: int32 [2048], P('group'), parts along dimension 0, may hold values from 0 to 1023, each once
Outputs:
- beam_power: bfloat16 [2048, 16, 128], P(('group', 'chan')), parts along dimension 0
- solved_gains: float32 [32, 4, 512], P(('group', 'chan')), parts along dimension 0
The draws below stay inside these ranges and needn't reach their ends.
There are 2 independent parts, one for each index of `group`. The reference program is written for one: setup_inputs(seed, part) draws one part's arguments, and reference() takes and returns one part's arrays. A program takes and returns all parts, laid end to end along the dimension named above; an argument that names none is the same for every part. Nothing has to cross between parts.
Inputs may be any that keep to these rules, and one draw needn't show every extreme that they name: `pointing`: each table direction is named by exactly one beam.
All inputs are finite; a program needn't handle non-finite values. No bound on the sum of `flags` on one device may be relied on, other than what follows from the above.
Results may differ from the reference program's by a relative error of at most 0.004.
Values may be sent and summed in bfloat16 or wider, within the bound.
A program may use at most 64 MiB of HBM per device.

```python
import math
import jax
import jax.numpy as jnp
from jax import lax

S = 512
BEAMS = 1024
NDIR = 1024
K = 4
ITERS = 8
TIME = 256
CHANNELS = 16


def set_ends(entries, stream_key, low, top_value):
    index_at = [jax.random.randint(jax.random.fold_in(stream_key, axis), (), 0, length) for axis, length in enumerate(entries.shape)]
    longest = entries.shape.index(max(entries.shape))
    beside = index_at[:longest] + [(index_at[longest] + 1) % entries.shape[longest]] + index_at[longest + 1:]
    return entries.at[tuple(index_at)].set(low).at[tuple(beside)].set(top_value)


def levels(own_key, shape, cuts, low, largest):
    def one(axis_at, parts):
        heights = jax.random.uniform(jax.random.fold_in(jax.random.fold_in(own_key, 6), axis_at), (parts,), jnp.float32, low / len(cuts), largest / len(cuts))
        return jnp.repeat(jnp.exp(heights), shape[axis_at] // parts).reshape((-1,) + (1,) * (len(shape) - axis_at - 1))

    level = one(*cuts[0])
    for cut in cuts[1:]:
        level = level * one(*cut)
    return level


def gaussian(key, dims, scale, most, pieces=(), kind=jnp.bfloat16):
    result = scale * jax.random.normal(key, dims, jnp.float32)
    if pieces:
        result = result * levels(key, dims, pieces, -0.22, 0.18)
    return jnp.clip(result, -most, most).astype(kind)


def setup_inputs(seed: int = 0, part: int = 0) -> dict:
    streams_of = jax.random.split(jax.random.key(seed), 8)
    part_keys = jax.random.split(jax.random.fold_in(streams_of[7], part), 8)
    return {
        "voltages": gaussian(part_keys[0], (CHANNELS, 2, TIME, 2 * S), 1.0, 6.0, ((0, 16),)),
        "cal_num": gaussian(part_keys[1], (CHANNELS, 4, S), 1.0, 6.0, ((0, 16),), jnp.float32),
        "cal_weight": jnp.clip(jnp.exp(math.log(5.0) - 3.218876 * jax.random.uniform(part_keys[2], (CHANNELS, 2, S), jnp.float32) ** levels(part_keys[2], (CHANNELS, 2, S), ((0, 16),), -0.2, 0.2)), 0.2, 5.0),
        "flags": set_ends((jax.random.randint(part_keys[3], (CHANNELS, S), 0, 8) < 7).astype(jnp.int32), jax.random.fold_in(part_keys[3], 1), 0, 1),
        "positions": jnp.clip(jax.random.uniform(streams_of[4], (2, S), jnp.float32, -300.0, 300.0), -300.0, 300.0),
        "directions": jnp.clip(jax.random.uniform(streams_of[5], (2, NDIR), jnp.float32, -0.05, 0.05), -0.05, 0.05),
        "pointing": jax.random.permutation(part_keys[6], BEAMS).astype(jnp.int32),
    }


PENALTY = 2.0
RIDGE = 1.0
TWO_PI = 6.283185307179586
HIGHEST = lax.Precision.HIGHEST


def basis_rows(channel_ids, total):
    place = 2.0 * (channel_ids.astype(jnp.float32) + 0.5) / total - 1.0
    return jnp.stack([jnp.ones_like(place), place, 0.5 * (3.0 * place * place - 1.0), 0.5 * (5.0 * place * place * place - 3.0 * place)], axis=1)


def invert_small(matrix):
    order = matrix.shape[0]
    unit = jnp.ones_like(matrix[0, 0])
    nothing = jnp.zeros_like(matrix[0, 0])
    left = [[matrix[row, column] for column in range(order)] for row in range(order)]
    right = [[unit if row == column else nothing for column in range(order)] for row in range(order)]
    for pivot in range(order):
        factor = 1.0 / left[pivot][pivot]
        left[pivot] = [entry * factor for entry in left[pivot]]
        right[pivot] = [entry * factor for entry in right[pivot]]
        for row in range(order):
            if row != pivot:
                scale = left[row][pivot]
                left[row] = [first - scale * second for first, second in zip(left[row], left[pivot])]
                right[row] = [first - scale * second for first, second in zip(right[row], right[pivot])]
    return jnp.stack([jnp.stack(line, 0) for line in right], 0)


def beam_detect(volts, fitted, usable, ratio, projected):
    phase = projected * (TWO_PI * ratio)
    cosine = jnp.cos(phase)
    sine = jnp.sin(phase)
    stations = projected.shape[1]
    beams = projected.shape[0]
    scale = usable * (stations ** -0.5)
    total = jnp.zeros((beams, volts.shape[1]), jnp.float32)
    for polar in range(2):
        gain_re = (fitted[2 * polar] * scale)[None, :]
        gain_im = (fitted[2 * polar + 1] * scale)[None, :]
        w_re = (gain_re * cosine - gain_im * sine).astype(jnp.bfloat16)
        w_im = (-(gain_re * sine + gain_im * cosine)).astype(jnp.bfloat16)
        upper = jnp.concatenate([w_re, -w_im], axis=1)
        lower = jnp.concatenate([w_im, w_re], axis=1)
        matrix = jnp.concatenate([upper, lower], axis=0)
        output = lax.dot_general(matrix, volts[polar], (((1,), (1,)), ((), ())), preferred_element_type=jnp.float32)
        total = total + output[:beams] * output[:beams] + output[beams:] * output[beams:]
    return total


def reference(voltages, cal_num, cal_weight, flags, positions, directions, pointing):
    channel_ids = jnp.arange(CHANNELS, dtype=jnp.int32)
    basis = basis_rows(channel_ids, CHANNELS)
    usable = flags.astype(jnp.float32)
    gram = jnp.einsum("ck,cj,cs->kjs", basis, basis, usable, precision=HIGHEST)
    identity = jnp.eye(K, dtype=jnp.float32)[:, :, None]
    inverse = invert_small(gram + RIDGE * identity)
    weight4 = jnp.repeat(cal_weight, 2, axis=1)
    mask = usable[:, None, :]
    fitted = jnp.zeros(cal_num.shape, jnp.float32)
    dual = jnp.zeros(cal_num.shape, jnp.float32)
    for sweep in range(ITERS):
        local = (mask * cal_num + PENALTY * (fitted - dual)) / (mask * weight4 + PENALTY)
        numerator = jnp.einsum("ck,cqs->kqs", basis, mask * (local + dual), precision=HIGHEST)
        coefficients = jnp.einsum("kjs,jqs->kqs", inverse, numerator, precision=HIGHEST)
        fitted = jnp.einsum("ck,kqs->cqs", basis, coefficients, precision=HIGHEST)
        dual = dual + mask * (local - fitted)
    east = directions[0][pointing]
    north = directions[1][pointing]
    projected = east[:, None] * positions[0][None, :] + north[:, None] * positions[1][None, :]
    ratio = 1.0 + 0.3 * (channel_ids.astype(jnp.float32) + 0.5) / CHANNELS

    def one_channel(items):
        volts, fit_one, usable_one, ratio_one = items
        power = beam_detect(volts, fit_one, usable_one, ratio_one, projected)
        return ((power[:, 0::2] + power[:, 1::2]) * 0.5).astype(jnp.bfloat16)

    detected = lax.map(one_channel, (voltages, fitted, usable, ratio))
    beam_power = jnp.transpose(detected, (1, 0, 2))
    return beam_power, fitted
```

```python
import functools
import jax
import jax.numpy as jnp
from jax import lax
from jax.experimental import pallas as pl
from jax.experimental.pallas import tpu as pltpu
from jax.sharding import PartitionSpec as P

ITERS = 8
PENALTY = 2.0
RIDGE = 1.0
ORDER = 4
LANES = 128
SINE = (4.44288292, -7.30824569, 3.60635422, -0.84611165, 0.10982452)
COSINE = (1.4142135, -6.97885095, 5.73946038, -1.88355791, 0.31068803)


def basis_at(place):
    return (
        1.0,
        place,
        0.5 * (3.0 * place * place - 1.0),
        0.5 * (5.0 * place * place * place - 3.0 * place),
    )


def invert_small(matrix):
    order = len(matrix)
    unit = jnp.ones_like(matrix[0][0])
    nothing = jnp.zeros_like(unit)
    left = [list(line) for line in matrix]
    right = [[unit if row == col else nothing for col in range(order)] for row in range(order)]
    for pivot in range(order):
        factor = 1.0 / left[pivot][pivot]
        left[pivot] = [entry * factor for entry in left[pivot]]
        right[pivot] = [entry * factor for entry in right[pivot]]
        for row in range(order):
            if row != pivot:
                scale = left[row][pivot]
                left[row] = [a - scale * b for a, b in zip(left[row], left[pivot])]
                right[row] = [a - scale * b for a, b in zip(right[row], right[pivot])]
    return right


def horner(coefficients, value):
    total = coefficients[-1] * value + coefficients[-2]
    for entry in coefficients[-3::-1]:
        total = total * value + entry
    return total


def tile_at(step, mine, tiles):
    if tiles == 4:
        high = lax.rem(mine // 2 + 1 - step // 2, 2)
        low = lax.rem(lax.rem(mine, 2) + (step + 1) // 2, 2)
        return 2 * high + low
    return lax.rem(mine + tiles // 2 + step, tiles)


def kernel(
    n,
    volts_ref,
    num_ref,
    weight_ref,
    flags_ref,
    positions_ref,
    directions_ref,
    pointing_ref,
    power_ref,
    gains_ref,
    gathered,
    volts,
    ordered,
    products,
    phasors,
    ready,
    columns,
    table,
    local_ref,
    dual_ref,
    volts_sem,
    cal_send,
    cal_recv,
    out_send,
    out_recv,
    own_sem,
):
    me = lax.axis_index("chan")
    stations = flags_ref.shape[1]
    blocks = stations // LANES
    tiles, depth, width = phasors.shape
    samples = volts.shape[1]
    half = samples // 2
    per_device = ready.shape[0] // n
    per_tile = n // tiles

    volts_copy = pltpu.make_async_copy(volts_ref.at[0], volts, volts_sem)
    volts_copy.start()

    barrier = pltpu.get_barrier_semaphore()

    @pl.loop(1, n)
    def _(offset):
        pl.semaphore_signal(
            barrier,
            inc=1,
            device_id={"chan": lax.rem(me + offset, n)},
            device_id_type=pl.DeviceIdType.MESH,
        )

    for block in range(blocks):
        lanes = pl.ds(block * LANES, LANES)
        mask = flags_ref[:, lanes].astype(jnp.float32)
        for polar in range(2):
            row = pl.ds(polar * blocks + block, 1)
            for part in range(2):
                gathered[me, part, row, :] = mask * num_ref[0, pl.ds(2 * polar + part, 1), lanes]
            gathered[me, 2, row, :] = mask * weight_ref[0, pl.ds(polar, 1), lanes]

    pl.semaphore_wait(barrier, n - 1)

    def cal_copy(slot, peer, sent, received):
        return pltpu.make_async_remote_copy(
            src_ref=gathered.at[slot],
            dst_ref=gathered.at[slot],
            send_sem=cal_send.at[sent],
            recv_sem=cal_recv.at[received],
            device_id={"chan": peer},
            device_id_type=pl.DeviceIdType.MESH,
        )

    @pl.loop(1, n)
    def _(offset):
        peer = lax.rem(me + offset, n)
        cal_copy(me, peer, peer, me).start()

    for axis in range(2):
        for block in range(blocks):
            lanes = pl.ds(block * LANES, LANES)
            row = jnp.broadcast_to(positions_ref[pl.ds(axis, 1), lanes], (LANES, LANES))
            columns[axis, lanes, :] = row.T

    rest = directions_ref[...]
    table[...] = jnp.zeros_like(table)
    for term in range(3):
        head = rest.astype(jnp.bfloat16).astype(jnp.float32)
        table[pl.ds(8 * term, 2), :] = head
        rest = rest - head
    terms = table[...].astype(jnp.bfloat16)
    place = 2.0 * (me.astype(jnp.float32) + 0.5) / n
    ratio = 1.0 + 0.15 * place
    entries = directions_ref.shape[1]
    chunk = 64

    @pl.loop(0, tiles)
    def _(tile):
        wanted = pointing_ref[tile]
        numbers = lax.broadcasted_iota(jnp.int32, (entries, width), 0)
        chosen = jnp.where(numbers == wanted, 1.0, 0.0).astype(jnp.bfloat16)
        found = jnp.dot(terms, chosen, preferred_element_type=jnp.float32)
        pointed = (found[0:8] + found[8:16] + found[16:24]) * ratio
        east = pointed[0:1]
        north = pointed[1:2]

        @pl.loop(0, stations // chunk)
        def _(step):
            rows = pl.ds(pl.multiple_of(step * chunk, chunk), chunk)
            below = pl.ds(pl.multiple_of(stations + step * chunk, chunk), chunk)
            for piece in range(width // LANES):
                lanes = pl.ds(piece * LANES, LANES)
                cut = slice(piece * LANES, (piece + 1) * LANES)
                turns = columns[0, rows, :] * east[:, cut] + columns[1, rows, :] * north[:, cut]
                turns = turns - jnp.round(turns)
                square = turns * turns
                sine = horner(SINE, square) * turns
                cosine = horner(COSINE, square)
                phasors[tile, rows, lanes] = (1.0 - sine * sine).astype(jnp.bfloat16)
                phasors[tile, below, lanes] = (sine * cosine).astype(jnp.bfloat16)

    volts_copy.wait()
    row = lax.broadcasted_iota(jnp.int32, (samples, samples), 0)
    col = lax.broadcasted_iota(jnp.int32, (samples, samples), 1)
    origin = jnp.where(row < half, 2 * row, 2 * (row - half) + 1)
    shuffle = jnp.where(col == origin, 1.0, 0.0).astype(jnp.bfloat16)
    for polar in range(2):
        ordered[polar] = jnp.dot(shuffle, volts[polar], preferred_element_type=jnp.float32)

    @pl.loop(1, n)
    def _(offset):
        peer = lax.rem(me + offset, n)
        cal_copy(peer, peer, peer, peer).wait_recv()

    basis = [basis_at(2.0 * (channel + 0.5) / n - 1.0) for channel in range(n)]
    nothing = jnp.zeros(gathered.shape[2:], jnp.float32)
    gram = [[nothing] * ORDER for _ in range(ORDER)]
    for channel in range(n):
        usable = jnp.where(gathered[channel, 2] > 0.0, 1.0, 0.0)
        for first in range(ORDER):
            for second in range(first, ORDER):
                factor = basis[channel][first] * basis[channel][second]
                gram[first][second] = gram[first][second] + factor * usable
    for first in range(ORDER):
        gram[first][first] = gram[first][first] + RIDGE
        for second in range(first):
            gram[first][second] = gram[second][first]
    inverse = invert_small(gram)
    local_ref[...] = jnp.zeros_like(local_ref)
    dual_ref[...] = jnp.zeros_like(dual_ref)

    def sweep(_, coefficients):
        numerator = [[nothing] * ORDER for _ in range(2)]
        for channel in range(n):
            values = basis[channel]
            weight = gathered[channel, 2]
            usable = jnp.where(weight > 0.0, 1.0, 0.0)
            damping = 1.0 / (weight + PENALTY)
            for part in range(2):
                line = coefficients[part]
                fitted = line[0]
                for term in range(1, ORDER):
                    fitted = fitted + values[term] * line[term]
                dual = dual_ref[channel, part]
                dual = dual + usable * (local_ref[channel, part] - fitted)
                local = (gathered[channel, part] + PENALTY * (fitted - dual)) * damping
                local_ref[channel, part] = local
                dual_ref[channel, part] = dual
                share = usable * (local + dual)
                numerator[part] = [
                    total + value * share for total, value in zip(numerator[part], values)
                ]
        result = []
        for part in range(2):
            line = []
            for first in range(ORDER):
                total = inverse[first][0] * numerator[part][0]
                for second in range(1, ORDER):
                    total = total + inverse[first][second] * numerator[part][second]
                line.append(total)
            result.append(tuple(line))
        return tuple(result)

    start = tuple(tuple(nothing for _ in range(ORDER)) for _ in range(2))
    coefficients = lax.fori_loop(0, ITERS, sweep, start)
    own = basis_at(place - 1.0)
    for part in range(2):
        fitted = coefficients[part][0]
        for term in range(1, ORDER):
            fitted = fitted + own[term] * coefficients[part][term]
        for polar in range(2):
            for block in range(blocks):
                at = polar * blocks + block
                lanes = pl.ds(block * LANES, LANES)
                gains_ref[0, pl.ds(2 * polar + part, 1), lanes] = fitted[at : at + 1]

    scale = flags_ref[...].astype(jnp.float32) * stations ** (-0.5)
    strip = 64
    for polar in range(2):
        gain_re = gains_ref[0, pl.ds(2 * polar, 1), :] * scale
        gain_im = gains_ref[0, pl.ds(2 * polar + 1, 1), :] * scale

        @pl.loop(0, samples // strip)
        def _(step):
            rows = pl.ds(pl.multiple_of(step * strip, strip), strip)
            real = ordered[polar, rows, :stations]
            imag = ordered[polar, rows, stations:]
            new_re = (gain_re * real + gain_im * imag).astype(jnp.bfloat16)
            new_im = (gain_re * imag - gain_im * real).astype(jnp.bfloat16)
            upper = pl.ds(pl.multiple_of(2 * polar * samples + step * strip, strip), strip)
            lower = pl.ds(pl.multiple_of((2 * polar + 1) * samples + step * strip, strip), strip)
            products[upper, :stations] = new_re
            products[upper, stations:] = new_im
            products[lower, :stations] = new_im
            products[lower, stations:] = -new_re

    def out_copy(owner, source, sent, received):
        rows = pl.ds(pl.multiple_of(owner * per_device, per_device), per_device)
        return pltpu.make_async_remote_copy(
            src_ref=ready.at[rows, :],
            dst_ref=power_ref.at[source],
            send_sem=out_send.at[sent],
            recv_sem=out_recv.at[received],
            device_id={"chan": owner},
            device_id_type=pl.DeviceIdType.MESH,
        )

    def own_copy():
        rows = pl.ds(pl.multiple_of(me * per_device, per_device), per_device)
        return pltpu.make_async_copy(ready.at[rows, :], power_ref.at[me], own_sem)

    @pl.loop(0, tiles)
    def _(step):
        tile = tile_at(step, me // per_tile, tiles)
        beams = jnp.dot(products[...], phasors[tile], preferred_element_type=jnp.float32)
        total = beams[:samples] * beams[:samples]
        for part in range(1, 4):
            piece = beams[part * samples : (part + 1) * samples]
            total = total + piece * piece
        mean = (total[:half] + total[half:]) * 0.5
        rows = pl.ds(pl.multiple_of(tile * width, width), width)
        ready[rows, :] = mean.T.astype(jnp.bfloat16)

        @pl.loop(0, per_tile)
        def _(index):
            owner = tile * per_tile + index

            @pl.when(owner != me)
            def _():
                out_copy(owner, me, owner, me).start()

            @pl.when(owner == me)
            def _():
                own_copy().start()

    own_copy().wait()

    @pl.loop(1, n)
    def _(offset):
        peer = lax.rem(me + offset, n)
        cal_copy(me, peer, peer, me).wait_send()
        out_copy(peer, me, peer, me).wait_send()
        out_copy(peer, peer, peer, peer).wait_recv()


def body(voltages, cal_num, cal_weight, flags, positions, directions, pointing):
    n = lax.axis_size("chan")
    count, polars, samples, depth = voltages.shape
    assert count == 1 and polars == 2
    stations = flags.shape[1]
    blocks = stations // LANES
    beams = pointing.shape[0]
    tiles = 4
    width = beams // tiles
    per_device = beams // n
    half = samples // 2
    entries = directions.shape[1]
    vmem = pl.BlockSpec(memory_space=pltpu.VMEM)
    anywhere = pl.BlockSpec(memory_space=pl.ANY)
    power, gains = pl.pallas_call(
        functools.partial(kernel, n),
        out_shape=(
            jax.ShapeDtypeStruct((n, per_device, half), jnp.bfloat16),
            jax.ShapeDtypeStruct(cal_num.shape, jnp.float32),
        ),
        in_specs=[anywhere] + [vmem] * 6,
        out_specs=(anywhere, vmem),
        scratch_shapes=[
            pltpu.VMEM((n, 3, 2 * blocks, LANES), jnp.float32),
            pltpu.VMEM((polars, samples, depth), jnp.bfloat16),
            pltpu.VMEM((polars, samples, depth), jnp.float32),
            pltpu.VMEM((4 * samples, depth), jnp.bfloat16),
            pltpu.VMEM((tiles, depth, width), jnp.bfloat16),
            pltpu.VMEM((beams, half), jnp.bfloat16),
            pltpu.VMEM((2, stations, LANES), jnp.float32),
            pltpu.VMEM((32, entries), jnp.float32),
            pltpu.VMEM((n, 2, 2 * blocks, LANES), jnp.float32),
            pltpu.VMEM((n, 2, 2 * blocks, LANES), jnp.float32),
            pltpu.SemaphoreType.DMA,
            pltpu.SemaphoreType.DMA((n,)),
            pltpu.SemaphoreType.DMA((n,)),
            pltpu.SemaphoreType.DMA((n,)),
            pltpu.SemaphoreType.DMA((n,)),
            pltpu.SemaphoreType.DMA,
        ],
        compiler_params=pltpu.CompilerParams(
            collective_id=0, has_side_effects=True, vmem_limit_bytes=40 * 2**20
        ),
    )(
        voltages,
        cal_num,
        cal_weight,
        flags,
        positions,
        directions,
        pointing.reshape(tiles, 1, width),
    )
    return jnp.transpose(power, (1, 0, 2)), gains


def solution(mesh):
    return jax.shard_map(
        body,
        mesh=mesh,
        in_specs=(
            P(("group", "chan"), None, None, None),
            P(("group", "chan"), None, None),
            P(("group", "chan"), None, None),
            P(("group", "chan"), None),
            P(),
            P(),
            P("group"),
        ),
        out_specs=(P(("group", "chan"), None, None), P(("group", "chan"), None, None)),
        check_vma=False,
    )
```

```python
import functools
import jax
import jax.numpy as jnp
from jax import lax
from jax.experimental import pallas as pl
from jax.experimental.pallas import tpu as pltpu
from jax.sharding import PartitionSpec as P

ITERS = 8
PENALTY = 2.0
RIDGE = 1.0
ORDER = 4
LANES = 128
SINE = (4.44288292, -7.30824569, 3.60635422, -0.84611165, 0.10982452)
COSINE = (1.4142135, -6.97885095, 5.73946038, -1.88355791, 0.31068803)


def basis_at(place):
    return (
        1.0,
        place,
        0.5 * (3.0 * place * place - 1.0),
        0.5 * (5.0 * place * place * place - 3.0 * place),
    )


def invert_small(matrix):
    order = len(matrix)
    unit = jnp.ones_like(matrix[0][0])
    nothing = jnp.zeros_like(unit)
    left = [list(line) for line in matrix]
    right = [[unit if row == col else nothing for col in range(order)] for row in range(order)]
    for pivot in range(order):
        factor = 1.0 / left[pivot][pivot]
        left[pivot] = [entry * factor for entry in left[pivot]]
        right[pivot] = [entry * factor for entry in right[pivot]]
        for row in range(order):
            if row != pivot:
                scale = left[row][pivot]
                left[row] = [a - scale * b for a, b in zip(left[row], left[pivot])]
                right[row] = [a - scale * b for a, b in zip(right[row], right[pivot])]
    return right


def horner(coefficients, value):
    total = coefficients[-1] * value + coefficients[-2]
    for entry in coefficients[-3::-1]:
        total = total * value + entry
    return total


def tile_at(step, mine, tiles):
    if tiles == 4:
        high = lax.rem(mine // 2 + 1 - step // 2, 2)
        low = lax.rem(lax.rem(mine, 2) + (step + 1) // 2, 2)
        return 2 * high + low
    return lax.rem(mine + tiles // 2 + step, tiles)


def combine(factors, terms):
    total = terms[0] * factors[0]
    for factor, term in zip(factors[1:], terms[1:]):
        total = total + factor * term
    return total


def tree(terms):
    while len(terms) > 1:
        terms = [sum(terms[at : at + 2]) if at + 1 < len(terms) else terms[at] for at in range(0, len(terms), 2)]
    return terms[0]


def kernel(
    n,
    tiles,
    volts_hbm,
    num_hbm,
    weight_hbm,
    flags_hbm,
    positions_hbm,
    directions_hbm,
    pointing_hbm,
    power_ref,
    gains_ref,
    num_ref,
    weight_ref,
    flags_ref,
    positions_ref,
    directions_ref,
    pointing_ref,
    volts,
    message,
    gathered,
    outbox,
    inbox,
    ordered,
    products,
    phasors,
    ready,
    columns,
    table,
    local_ref,
    dual_ref,
    load_sem,
    cal_send,
    cal_recv,
    fit_send,
    fit_recv,
    out_send,
    out_recv,
    own_sem,
):
    me = lax.axis_index("chan")
    stations = flags_ref.shape[1]
    blocks = stations // LANES
    width = phasors.shape[2]
    samples = volts.shape[1]
    half = samples // 2
    per_device = ready.shape[0] // n
    per_tile = n // tiles
    share = lax.rem(me, blocks)

    loads = [
        pltpu.make_async_copy(source, target, load_sem.at[index])
        for index, (source, target) in enumerate(
            (
                (num_hbm.at[0], num_ref),
                (weight_hbm.at[0], weight_ref),
                (flags_hbm, flags_ref),
                (positions_hbm, positions_ref),
                (directions_hbm, directions_ref),
                (pointing_hbm, pointing_ref),
                (volts_hbm.at[0], volts),
            )
        )
    ]
    for load in loads:
        load.start()

    barrier = pltpu.get_barrier_semaphore()

    @pl.loop(1, n)
    def _(offset):
        pl.semaphore_signal(
            barrier,
            inc=1,
            device_id={"chan": lax.rem(me + offset, n)},
            device_id_type=pl.DeviceIdType.MESH,
        )

    for load in loads[:3]:
        load.wait()
    for block in range(blocks):
        lanes = pl.ds(block * LANES, LANES)
        mask = flags_ref[:, lanes].astype(jnp.float32)
        message[block, 0:4, :] = mask * num_ref[:, lanes]
        for row in range(4):
            message[block, pl.ds(4 + row, 1), :] = mask * weight_ref[pl.ds(row // 2, 1), lanes]
    gathered[me] = message[share]

    pl.semaphore_wait(barrier, n - 1)

    def cal_copy(block, slot, peer, sent, received):
        return pltpu.make_async_remote_copy(
            src_ref=message.at[block],
            dst_ref=gathered.at[slot],
            send_sem=cal_send.at[sent],
            recv_sem=cal_recv.at[received],
            device_id={"chan": peer},
            device_id_type=pl.DeviceIdType.MESH,
        )

    @pl.loop(1, n)
    def _(offset):
        peer = lax.rem(me + offset, n)
        cal_copy(lax.rem(peer, blocks), me, peer, peer, me).start()

    for load in loads[3:6]:
        load.wait()
    for axis in range(2):
        for block in range(blocks):
            lanes = pl.ds(block * LANES, LANES)
            row = jnp.broadcast_to(positions_ref[pl.ds(axis, 1), lanes], (LANES, LANES))
            columns[axis, lanes, :] = row.T

    rest = directions_ref[...]
    table[...] = jnp.zeros_like(table)
    for term in range(3):
        head = rest.astype(jnp.bfloat16).astype(jnp.float32)
        table[pl.ds(8 * term, 2), :] = head
        rest = rest - head
    ratio = 1.0 + 0.15 * (2.0 * (me.astype(jnp.float32) + 0.5) / n)
    entries = directions_ref.shape[1]
    chunk = 64

    def make_phasors(step):
        wanted = pointing_ref[tile_at(step, me // per_tile, tiles)]
        numbers = lax.broadcasted_iota(jnp.int32, (entries, width), 0)
        chosen = jnp.where(numbers == wanted, 1.0, 0.0).astype(jnp.bfloat16)
        terms = table[...].astype(jnp.bfloat16)
        found = jnp.dot(terms, chosen, preferred_element_type=jnp.float32)
        pointed = (found[0:8] + found[8:16] + found[16:24]) * ratio
        east = pointed[0:1]
        north = pointed[1:2]

        @pl.loop(0, stations // chunk)
        def _(part):
            rows = pl.ds(pl.multiple_of(part * chunk, chunk), chunk)
            below = pl.ds(pl.multiple_of(stations + part * chunk, chunk), chunk)
            for piece in range(width // LANES):
                lanes = pl.ds(piece * LANES, LANES)
                cut = slice(piece * LANES, (piece + 1) * LANES)
                turns = columns[0, rows, :] * east[:, cut] + columns[1, rows, :] * north[:, cut]
                turns = turns - jnp.round(turns)
                square = turns * turns
                sine = horner(SINE, square) * turns
                cosine = horner(COSINE, square)
                phasors[step, rows, lanes] = (1.0 - sine * sine).astype(jnp.bfloat16)
                phasors[step, below, lanes] = (sine * cosine).astype(jnp.bfloat16)

    make_phasors(0)

    loads[6].wait()
    row = lax.broadcasted_iota(jnp.int32, (samples, samples), 0)
    col = lax.broadcasted_iota(jnp.int32, (samples, samples), 1)
    origin = jnp.where(row < half, 2 * row, 2 * (row - half) + 1)
    shuffle = jnp.where(col == origin, 1.0, 0.0).astype(jnp.bfloat16)
    for polar in range(2):
        ordered[polar] = jnp.dot(shuffle, volts[polar], preferred_element_type=jnp.float32)

    @pl.loop(1, n)
    def _(offset):
        peer = lax.rem(me + offset, n)
        cal_copy(0, peer, peer, peer, peer).wait_recv()

    basis = [basis_at(2.0 * (channel + 0.5) / n - 1.0) for channel in range(n)]
    nothing = jnp.zeros((4, LANES), jnp.float32)
    gram = [[nothing] * ORDER for _ in range(ORDER)]
    for channel in range(n):
        usable = jnp.where(gathered[channel, 4:8] > 0.0, 1.0, 0.0)
        for first in range(ORDER):
            for second in range(first, ORDER):
                factor = basis[channel][first] * basis[channel][second]
                gram[first][second] = gram[first][second] + factor * usable
    for first in range(ORDER):
        gram[first][first] = gram[first][first] + RIDGE
        for second in range(first):
            gram[first][second] = gram[second][first]
    inverse = invert_small(gram)
    local_ref[...] = jnp.zeros_like(local_ref)
    dual_ref[...] = jnp.zeros_like(dual_ref)

    def sweep(_, line):
        numerator = [[] for _ in range(ORDER)]
        for channel in range(n):
            values = basis[channel]
            weight = gathered[channel, 4:8]
            usable = jnp.where(weight > 0.0, 1.0, 0.0)
            damping = 1.0 / (weight + PENALTY)
            fitted = combine(values, line)
            dual = dual_ref[channel] + usable * (local_ref[channel] - fitted)
            local = (gathered[channel, 0:4] + PENALTY * (fitted - dual)) * damping
            local_ref[channel] = local
            dual_ref[channel] = dual
            summand = usable * (local + dual)
            for term in range(ORDER):
                numerator[term].append(values[term] * summand)
        sums = [tree(terms) for terms in numerator]
        return tuple(combine(inverse[first], sums) for first in range(ORDER))

    line = lax.fori_loop(0, ITERS, sweep, (nothing,) * ORDER)

    def fitted_at(channel):
        return combine(basis_at(2.0 * (channel.astype(jnp.float32) + 0.5) / n - 1.0), line)

    def fit_copy(source, slot, peer, sent, received):
        return pltpu.make_async_remote_copy(
            src_ref=outbox.at[source],
            dst_ref=inbox.at[slot],
            send_sem=fit_send.at[sent],
            recv_sem=fit_recv.at[received],
            device_id={"chan": peer},
            device_id_type=pl.DeviceIdType.MESH,
        )

    for offset in range(1, blocks):
        mate = lax.rem(share + offset, blocks)
        peer = me - share + mate
        outbox[mate] = fitted_at(peer)
        fit_copy(mate, share, peer, mate, share).start()
    inbox[share] = fitted_at(me)

    ahead = min(3, tiles)
    for step in range(1, ahead):
        make_phasors(step)

    for offset in range(1, blocks):
        mate = lax.rem(share + offset, blocks)
        fit_copy(mate, mate, me - share + mate, mate, mate).wait_recv()
    for block in range(blocks):
        gains_ref[0, :, pl.ds(block * LANES, LANES)] = inbox[block]

    scale = flags_ref[...].astype(jnp.float32) * stations ** (-0.5)
    strip = 64
    for polar in range(2):
        gain_re = gains_ref[0, pl.ds(2 * polar, 1), :] * scale
        gain_im = gains_ref[0, pl.ds(2 * polar + 1, 1), :] * scale

        @pl.loop(0, samples // strip)
        def _(step):
            rows = pl.ds(pl.multiple_of(step * strip, strip), strip)
            real = ordered[polar, rows, :stations]
            imag = ordered[polar, rows, stations:]
            new_re = (gain_re * real + gain_im * imag).astype(jnp.bfloat16)
            new_im = (gain_re * imag - gain_im * real).astype(jnp.bfloat16)
            upper = pl.ds(pl.multiple_of(2 * polar * samples + step * strip, strip), strip)
            lower = pl.ds(pl.multiple_of((2 * polar + 1) * samples + step * strip, strip), strip)
            products[upper, :stations] = new_re
            products[upper, stations:] = new_im
            products[lower, :stations] = new_im
            products[lower, stations:] = -new_re

    def out_copy(owner, source, sent, received):
        rows = pl.ds(pl.multiple_of(owner * per_device, per_device), per_device)
        return pltpu.make_async_remote_copy(
            src_ref=ready.at[rows, :],
            dst_ref=power_ref.at[source],
            send_sem=out_send.at[sent],
            recv_sem=out_recv.at[received],
            device_id={"chan": owner},
            device_id_type=pl.DeviceIdType.MESH,
        )

    def own_copy():
        rows = pl.ds(pl.multiple_of(me * per_device, per_device), per_device)
        return pltpu.make_async_copy(ready.at[rows, :], power_ref.at[me], own_sem)

    @pl.loop(0, tiles)
    def _(step):
        tile = tile_at(step, me // per_tile, tiles)
        beams = jnp.dot(products[...], phasors[step], preferred_element_type=jnp.float32)
        total = beams[:samples] * beams[:samples]
        for part in range(1, 4):
            piece = beams[part * samples : (part + 1) * samples]
            total = total + piece * piece
        mean = (total[:half] + total[half:]) * 0.5
        rows = pl.ds(pl.multiple_of(tile * width, width), width)
        ready[rows, :] = mean.T.astype(jnp.bfloat16)

        @pl.loop(0, per_tile)
        def _(index):
            owner = tile * per_tile + index

            @pl.when(owner != me)
            def _():
                out_copy(owner, me, owner, me).start()

            @pl.when(owner == me)
            def _():
                own_copy().start()

        @pl.when(step < tiles - ahead)
        def _():
            make_phasors(step + ahead)

    own_copy().wait()
    for offset in range(1, blocks):
        mate = lax.rem(share + offset, blocks)
        fit_copy(mate, share, me - share + mate, mate, share).wait_send()

    @pl.loop(1, n)
    def _(offset):
        peer = lax.rem(me + offset, n)
        cal_copy(lax.rem(peer, blocks), me, peer, peer, me).wait_send()
        out_copy(peer, me, peer, me).wait_send()
        out_copy(peer, peer, peer, peer).wait_recv()


def body(voltages, cal_num, cal_weight, flags, positions, directions, pointing):
    n = lax.axis_size("chan")
    count, polars, samples, depth = voltages.shape
    stations = flags.shape[1]
    blocks = stations // LANES
    assert count == 1 and polars == 2 and n % blocks == 0
    beams = pointing.shape[0]
    tiles = 4
    width = beams // tiles
    half = samples // 2
    entries = directions.shape[1]
    vmem = pl.BlockSpec(memory_space=pltpu.VMEM)
    anywhere = pl.BlockSpec(memory_space=pl.ANY)
    hbm = pl.BlockSpec(memory_space=pltpu.HBM)
    f32 = jnp.float32
    power, gains = pl.pallas_call(
        functools.partial(kernel, n, tiles),
        out_shape=(
            jax.ShapeDtypeStruct((n, beams // n, half), jnp.bfloat16),
            jax.ShapeDtypeStruct(cal_num.shape, f32),
        ),
        in_specs=[hbm] * 7,
        out_specs=(anywhere, vmem),
        scratch_shapes=[
            pltpu.VMEM(cal_num.shape[1:], f32),
            pltpu.VMEM(cal_weight.shape[1:], f32),
            pltpu.VMEM(flags.shape, jnp.int32),
            pltpu.VMEM(positions.shape, f32),
            pltpu.VMEM(directions.shape, f32),
            pltpu.VMEM((tiles, 1, width), jnp.int32),
            pltpu.VMEM((polars, samples, depth), jnp.bfloat16),
            pltpu.VMEM((blocks, 8, LANES), f32),
            pltpu.VMEM((n, 8, LANES), f32),
            pltpu.VMEM((blocks, 4, LANES), f32),
            pltpu.VMEM((blocks, 4, LANES), f32),
            pltpu.VMEM((polars, samples, depth), f32),
            pltpu.VMEM((4 * samples, depth), jnp.bfloat16),
            pltpu.VMEM((tiles, depth, width), jnp.bfloat16),
            pltpu.VMEM((beams, half), jnp.bfloat16),
            pltpu.VMEM((2, stations, LANES), f32),
            pltpu.VMEM((32, entries), f32),
            pltpu.VMEM((n, 4, LANES), f32),
            pltpu.VMEM((n, 4, LANES), f32),
            pltpu.SemaphoreType.DMA((7,)),
            pltpu.SemaphoreType.DMA((n,)),
            pltpu.SemaphoreType.DMA((n,)),
            pltpu.SemaphoreType.DMA((blocks,)),
            pltpu.SemaphoreType.DMA((blocks,)),
            pltpu.SemaphoreType.DMA((n,)),
            pltpu.SemaphoreType.DMA((n,)),
            pltpu.SemaphoreType.DMA,
        ],
        compiler_params=pltpu.CompilerParams(
            collective_id=0, has_side_effects=True, vmem_limit_bytes=63 * 2**20
        ),
    )(
        voltages,
        cal_num,
        cal_weight,
        flags,
        positions,
        directions,
        pointing.reshape(tiles, 1, width),
    )
    return jnp.transpose(power, (1, 0, 2)), gains


def solution(mesh):
    return jax.shard_map(
        body,
        mesh=mesh,
        in_specs=(
            P(("group", "chan"), None, None, None),
            P(("group", "chan"), None, None),
            P(("group", "chan"), None, None),
            P(("group", "chan"), None),
            P(),
            P(),
            P("group"),
        ),
        out_specs=(P(("group", "chan"), None, None), P(("group", "chan"), None, None)),
        check_vma=False,
    )
```

```python
import functools
import jax
import jax.numpy as jnp
from jax import lax
from jax.experimental import pallas as pl
from jax.experimental.pallas import tpu as pltpu
from jax.sharding import PartitionSpec as P

ITERS = 8
PENALTY = 2.0
RIDGE = 1.0
ORDER = 4
LANES = 128
ROUNDING = 1.5 * 2.0**23
SINE = (4.44288292, -7.30824569, 3.60635422, -0.84611165, 0.10982452)
COSINE = (1.4142135, -6.97885095, 5.73946038, -1.88355791, 0.31068803)


def basis_at(place):
    return (
        1.0,
        place,
        0.5 * (3.0 * place * place - 1.0),
        0.5 * (5.0 * place * place * place - 3.0 * place),
    )


def invert_small(matrix):
    order = len(matrix)
    unit = jnp.ones_like(matrix[0][0])
    nothing = jnp.zeros_like(unit)
    left = [list(line) for line in matrix]
    right = [[unit if row == col else nothing for col in range(order)] for row in range(order)]
    for pivot in range(order):
        factor = 1.0 / left[pivot][pivot]
        left[pivot] = [entry * factor for entry in left[pivot]]
        right[pivot] = [entry * factor for entry in right[pivot]]
        for row in range(order):
            if row != pivot:
                scale = left[row][pivot]
                left[row] = [a - scale * b for a, b in zip(left[row], left[pivot])]
                right[row] = [a - scale * b for a, b in zip(right[row], right[pivot])]
    return right


def horner(coefficients, value):
    total = coefficients[-1] * value + coefficients[-2]
    for entry in coefficients[-3::-1]:
        total = total * value + entry
    return total


def tile_at(step, mine, tiles):
    if tiles == 4:
        high = lax.rem(mine // 2 + 1 - step // 2, 2)
        low = lax.rem(lax.rem(mine, 2) + (step + 1) // 2, 2)
        return 2 * high + low
    return lax.rem(mine + tiles // 2 + step, tiles)


def combine(factors, terms):
    total = terms[0] * factors[0]
    for factor, term in zip(factors[1:], terms[1:]):
        total = total + factor * term
    return total


def tree(terms):
    while len(terms) > 1:
        terms = [sum(terms[at : at + 2]) if at + 1 < len(terms) else terms[at] for at in range(0, len(terms), 2)]
    return terms[0]


def kernel(
    n,
    tiles,
    volts_hbm,
    num_hbm,
    weight_hbm,
    flags_hbm,
    positions_hbm,
    directions_hbm,
    pointing_hbm,
    power_ref,
    gains_ref,
    num_ref,
    weight_ref,
    flags_ref,
    positions_ref,
    directions_ref,
    pointing_ref,
    volts,
    message,
    gathered,
    outbox,
    inbox,
    ordered,
    products,
    phasors,
    ready,
    columns,
    table,
    local_ref,
    dual_ref,
    load_sem,
    cal_send,
    cal_recv,
    fit_send,
    fit_recv,
    out_send,
    out_recv,
    own_sem,
):
    me = lax.axis_index("chan")
    stations = flags_ref.shape[1]
    blocks = stations // LANES
    width = phasors.shape[2]
    samples = volts.shape[1]
    half = samples // 2
    per_device = ready.shape[0] // n
    per_tile = n // tiles
    share = lax.rem(me, blocks)

    loads = [
        pltpu.make_async_copy(source, target, load_sem.at[index])
        for index, (source, target) in enumerate(
            (
                (num_hbm.at[0], num_ref),
                (weight_hbm.at[0], weight_ref),
                (flags_hbm, flags_ref),
                (positions_hbm, positions_ref),
                (directions_hbm, directions_ref),
                (pointing_hbm, pointing_ref),
                (volts_hbm.at[0], volts),
            )
        )
    ]
    for load in loads:
        load.start()

    barrier = pltpu.get_barrier_semaphore()

    @pl.loop(1, n)
    def _(offset):
        pl.semaphore_signal(
            barrier,
            inc=1,
            device_id={"chan": lax.rem(me + offset, n)},
            device_id_type=pl.DeviceIdType.MESH,
        )

    for load in loads[:3]:
        load.wait()
    for block in range(blocks):
        lanes = pl.ds(block * LANES, LANES)
        mask = flags_ref[:, lanes].astype(jnp.float32)
        message[block, 0:4, :] = mask * num_ref[:, lanes]
        for row in range(4):
            message[block, pl.ds(4 + row, 1), :] = mask * weight_ref[pl.ds(row // 2, 1), lanes]
    gathered[me] = message[share]

    pl.semaphore_wait(barrier, n - 1)

    def cal_copy(block, slot, peer, sent, received):
        return pltpu.make_async_remote_copy(
            src_ref=message.at[block],
            dst_ref=gathered.at[slot],
            send_sem=cal_send.at[sent],
            recv_sem=cal_recv.at[received],
            device_id={"chan": peer},
            device_id_type=pl.DeviceIdType.MESH,
        )

    @pl.loop(1, n)
    def _(offset):
        peer = lax.rem(me + offset, n)
        cal_copy(lax.rem(peer, blocks), me, peer, peer, me).start()

    for load in loads[3:6]:
        load.wait()
    for axis in range(2):
        for block in range(blocks):
            lanes = pl.ds(block * LANES, LANES)
            row = jnp.broadcast_to(positions_ref[pl.ds(axis, 1), lanes], (LANES, LANES))
            columns[axis, lanes, :] = row.T

    rest = directions_ref[...]
    table[...] = jnp.zeros_like(table)
    for term in range(3):
        head = rest.astype(jnp.bfloat16).astype(jnp.float32)
        table[pl.ds(8 * term, 2), :] = head
        rest = rest - head
    ratio = 1.0 + 0.15 * (2.0 * (me.astype(jnp.float32) + 0.5) / n)
    entries = directions_ref.shape[1]
    chunk = 64

    def make_phasors(step):
        wanted = pointing_ref[tile_at(step, me // per_tile, tiles)]
        numbers = lax.broadcasted_iota(jnp.int32, (entries, width), 0)
        chosen = jnp.where(numbers == wanted, 1.0, 0.0).astype(jnp.bfloat16)
        terms = table[...].astype(jnp.bfloat16)
        found = jnp.dot(terms, chosen, preferred_element_type=jnp.float32)
        pointed = (found[0:8] + found[8:16] + found[16:24]) * ratio
        east = pointed[0:1]
        north = pointed[1:2]

        @pl.loop(0, stations // chunk)
        def _(part):
            rows = pl.ds(pl.multiple_of(part * chunk, chunk), chunk)
            below = pl.ds(pl.multiple_of(stations + part * chunk, chunk), chunk)
            for piece in range(width // LANES):
                lanes = pl.ds(piece * LANES, LANES)
                cut = slice(piece * LANES, (piece + 1) * LANES)
                turns = columns[0, rows, :] * east[:, cut] + columns[1, rows, :] * north[:, cut]
                turns = turns - ((turns + ROUNDING) - ROUNDING)
                square = turns * turns
                sine = horner(SINE, square) * turns
                cosine = horner(COSINE, square)
                phasors[step, rows, lanes] = (1.0 - sine * sine).astype(jnp.bfloat16)
                phasors[step, below, lanes] = (sine * cosine).astype(jnp.bfloat16)

    make_phasors(0)

    @pl.loop(1, n)
    def _(offset):
        peer = lax.rem(me + offset, n)
        cal_copy(0, peer, peer, peer, peer).wait_recv()

    pairs = n // 2
    basis = [basis_at(2.0 * (n - pair - 0.5) / n - 1.0) for pair in range(pairs)]
    sign = jnp.where(lax.broadcasted_iota(jnp.int32, (8, LANES), 0) < 4, 1.0, -1.0)
    solve_rows = []
    for pair in range(pairs):
        first = gathered[n - 1 - pair]
        second = gathered[pair]
        weight = jnp.concatenate([first[4:8], second[4:8]], axis=0)
        usable = jnp.where(weight > 0.0, 1.0, 0.0)
        damping = 1.0 / (weight + PENALTY)
        target = jnp.concatenate([first[0:4], second[0:4]], axis=0) * damping
        solve_rows.append((usable, PENALTY * damping, target))

    def both(term, value):
        value = value * sign if term % 2 else value
        return value + pltpu.roll(value, 4, 0)

    gram = [[None] * ORDER for _ in range(ORDER)]
    for first in range(ORDER):
        for second in range(first, ORDER):
            terms = [
                (basis[pair][first] * basis[pair][second]) * solve_rows[pair][0]
                for pair in range(pairs)
            ]
            gram[first][second] = both(first + second, tree(terms))
            gram[second][first] = gram[first][second]
        gram[first][first] = gram[first][first] + RIDGE
    inverse = invert_small(gram)
    local_ref[...] = jnp.zeros_like(local_ref)
    dual_ref[...] = jnp.zeros_like(dual_ref)
    nothing = jnp.zeros((8, LANES), jnp.float32)

    def sweep(_, line):
        signed = [entry * sign if term % 2 else entry for term, entry in enumerate(line)]
        numerator = [[] for _ in range(ORDER)]
        for pair in range(pairs):
            values = basis[pair]
            usable, damping, target = solve_rows[pair]
            fitted = tree([signed[0]] + [values[term] * signed[term] for term in range(1, ORDER)])
            dual = dual_ref[pair] + usable * (local_ref[pair] - fitted)
            local = target + damping * (fitted - dual)
            local_ref[pair] = local
            dual_ref[pair] = dual
            summand = usable * (local + dual)
            for term in range(ORDER):
                numerator[term].append(values[term] * summand if term else summand)
        sums = [both(term, tree(terms)) for term, terms in enumerate(numerator)]
        return tuple(
            tree([entry * total for entry, total in zip(inverse[first], sums)])
            for first in range(ORDER)
        )

    line = lax.fori_loop(0, ITERS, sweep, (nothing,) * ORDER)
    line = [entry[0:4] for entry in line]

    def fitted_at(channel):
        return combine(basis_at(2.0 * (channel.astype(jnp.float32) + 0.5) / n - 1.0), line)

    def fit_copy(source, slot, peer, sent, received):
        return pltpu.make_async_remote_copy(
            src_ref=outbox.at[source],
            dst_ref=inbox.at[slot],
            send_sem=fit_send.at[sent],
            recv_sem=fit_recv.at[received],
            device_id={"chan": peer},
            device_id_type=pl.DeviceIdType.MESH,
        )

    for offset in range(1, blocks):
        mate = lax.rem(share + offset, blocks)
        peer = me - share + mate
        outbox[mate] = fitted_at(peer)
        fit_copy(mate, share, peer, mate, share).start()
    inbox[share] = fitted_at(me)

    loads[6].wait()
    row = lax.broadcasted_iota(jnp.int32, (samples, samples), 0)
    col = lax.broadcasted_iota(jnp.int32, (samples, samples), 1)
    origin = jnp.where(row < half, 2 * row, 2 * (row - half) + 1)
    shuffle = jnp.where(col == origin, 1.0, 0.0).astype(jnp.bfloat16)
    for polar in range(2):
        ordered[polar] = jnp.dot(shuffle, volts[polar], preferred_element_type=jnp.float32)

    ahead = 1
    for offset in range(1, blocks):
        mate = lax.rem(share + offset, blocks)
        fit_copy(mate, mate, me - share + mate, mate, mate).wait_recv()
    for block in range(blocks):
        gains_ref[0, :, pl.ds(block * LANES, LANES)] = inbox[block]

    scale = flags_ref[...].astype(jnp.float32) * stations ** (-0.5)
    strip = 64
    for polar in range(2):
        gain_re = gains_ref[0, pl.ds(2 * polar, 1), :] * scale
        gain_im = gains_ref[0, pl.ds(2 * polar + 1, 1), :] * scale

        @pl.loop(0, samples // strip)
        def _(step):
            rows = pl.ds(pl.multiple_of(step * strip, strip), strip)
            real = ordered[polar, rows, :stations]
            imag = ordered[polar, rows, stations:]
            new_re = (gain_re * real + gain_im * imag).astype(jnp.bfloat16)
            new_im = (gain_re * imag - gain_im * real).astype(jnp.bfloat16)
            upper = pl.ds(pl.multiple_of(2 * polar * samples + step * strip, strip), strip)
            lower = pl.ds(pl.multiple_of((2 * polar + 1) * samples + step * strip, strip), strip)
            products[upper, :stations] = new_re
            products[upper, stations:] = new_im
            products[lower, :stations] = new_im
            products[lower, stations:] = -new_re

    def out_copy(owner, source, sent, received):
        rows = pl.ds(pl.multiple_of(owner * per_device, per_device), per_device)
        return pltpu.make_async_remote_copy(
            src_ref=ready.at[rows, :],
            dst_ref=power_ref.at[source],
            send_sem=out_send.at[sent],
            recv_sem=out_recv.at[received],
            device_id={"chan": owner},
            device_id_type=pl.DeviceIdType.MESH,
        )

    def own_copy():
        rows = pl.ds(pl.multiple_of(me * per_device, per_device), per_device)
        return pltpu.make_async_copy(ready.at[rows, :], power_ref.at[me], own_sem)

    @pl.loop(0, tiles)
    def _(step):
        tile = tile_at(step, me // per_tile, tiles)
        beams = jnp.dot(products[...], phasors[step], preferred_element_type=jnp.float32)
        total = beams[:samples] * beams[:samples]
        for part in range(1, 4):
            piece = beams[part * samples : (part + 1) * samples]
            total = total + piece * piece
        mean = (total[:half] + total[half:]) * 0.5
        rows = pl.ds(pl.multiple_of(tile * width, width), width)
        ready[rows, :] = mean.T.astype(jnp.bfloat16)

        @pl.loop(0, per_tile)
        def _(index):
            owner = tile * per_tile + index

            @pl.when(owner != me)
            def _():
                out_copy(owner, me, owner, me).start()

            @pl.when(owner == me)
            def _():
                own_copy().start()

        @pl.when(step < tiles - ahead)
        def _():
            make_phasors(step + ahead)

    own_copy().wait()
    for offset in range(1, blocks):
        mate = lax.rem(share + offset, blocks)
        fit_copy(mate, share, me - share + mate, mate, share).wait_send()

    @pl.loop(1, n)
    def _(offset):
        peer = lax.rem(me + offset, n)
        cal_copy(lax.rem(peer, blocks), me, peer, peer, me).wait_send()
        out_copy(peer, me, peer, me).wait_send()
        out_copy(peer, peer, peer, peer).wait_recv()


def body(voltages, cal_num, cal_weight, flags, positions, directions, pointing):
    n = lax.axis_size("chan")
    count, polars, samples, depth = voltages.shape
    stations = flags.shape[1]
    blocks = stations // LANES
    assert count == 1 and polars == 2 and n % blocks == 0 and n % 2 == 0
    beams = pointing.shape[0]
    tiles = 4
    width = beams // tiles
    half = samples // 2
    entries = directions.shape[1]
    vmem = pl.BlockSpec(memory_space=pltpu.VMEM)
    hbm = pl.BlockSpec(memory_space=pltpu.HBM)
    f32 = jnp.float32
    power, gains = pl.pallas_call(
        functools.partial(kernel, n, tiles),
        out_shape=(
            pltpu.VMEM((n, beams // n, half), jnp.bfloat16),
            jax.ShapeDtypeStruct(cal_num.shape, f32),
        ),
        in_specs=[hbm] * 7,
        out_specs=(vmem, vmem),
        scratch_shapes=[
            pltpu.VMEM(cal_num.shape[1:], f32),
            pltpu.VMEM(cal_weight.shape[1:], f32),
            pltpu.VMEM(flags.shape, jnp.int32),
            pltpu.VMEM(positions.shape, f32),
            pltpu.VMEM(directions.shape, f32),
            pltpu.VMEM((tiles, 1, width), jnp.int32),
            pltpu.VMEM((polars, samples, depth), jnp.bfloat16),
            pltpu.VMEM((blocks, 8, LANES), f32),
            pltpu.VMEM((n, 8, LANES), f32),
            pltpu.VMEM((blocks, 4, LANES), f32),
            pltpu.VMEM((blocks, 4, LANES), f32),
            pltpu.VMEM((polars, samples, depth), f32),
            pltpu.VMEM((4 * samples, depth), jnp.bfloat16),
            pltpu.VMEM((tiles, depth, width), jnp.bfloat16),
            pltpu.VMEM((beams, half), jnp.bfloat16),
            pltpu.VMEM((2, stations, LANES), f32),
            pltpu.VMEM((32, entries), f32),
            pltpu.VMEM((n // 2, 8, LANES), f32),
            pltpu.VMEM((n // 2, 8, LANES), f32),
            pltpu.SemaphoreType.DMA((7,)),
            pltpu.SemaphoreType.DMA((n,)),
            pltpu.SemaphoreType.DMA((n,)),
            pltpu.SemaphoreType.DMA((blocks,)),
            pltpu.SemaphoreType.DMA((blocks,)),
            pltpu.SemaphoreType.DMA((n,)),
            pltpu.SemaphoreType.DMA((n,)),
            pltpu.SemaphoreType.DMA,
        ],
        compiler_params=pltpu.CompilerParams(
            collective_id=0, has_side_effects=True, vmem_limit_bytes=40 * 2**20
        ),
    )(
        *(
            pltpu.with_memory_space_constraint(operand, pltpu.HBM)
            for operand in (
                voltages,
                cal_num,
                cal_weight,
                flags,
                positions,
                directions,
                pointing.reshape(tiles, 1, width),
            )
        )
    )
    return jnp.transpose(power, (1, 0, 2)), gains


def solution(mesh):
    return jax.shard_map(
        body,
        mesh=mesh,
        in_specs=(
            P(("group", "chan"), None, None, None),
            P(("group", "chan"), None, None),
            P(("group", "chan"), None, None),
            P(("group", "chan"), None),
            P(),
            P(),
            P("group"),
        ),
        out_specs=(P(("group", "chan"), None, None), P(("group", "chan"), None, None)),
        check_vma=False,
    )
```

```python
import functools
import jax
import jax.numpy as jnp
from jax import lax
from jax.experimental import pallas as pl
from jax.experimental.pallas import tpu as pltpu
from jax.sharding import PartitionSpec as P

ITERS = 8
PENALTY = 2.0
RIDGE = 1.0
ORDER = 4
LANES = 128
ROUNDING = 1.5 * 2.0**23
SINE = (4.44288292, -7.30824569, 3.60635422, -0.84611165, 0.10982452)
COSINE = (1.4142135, -6.97885095, 5.73946038, -1.88355791, 0.31068803)


def basis_at(place):
    return (
        1.0,
        place,
        0.5 * (3.0 * place * place - 1.0),
        0.5 * (5.0 * place * place * place - 3.0 * place),
    )


def invert_small(matrix):
    order = len(matrix)
    unit = jnp.ones_like(matrix[0][0])
    nothing = jnp.zeros_like(unit)
    left = [list(line) for line in matrix]
    right = [[unit if row == col else nothing for col in range(order)] for row in range(order)]
    for pivot in range(order):
        factor = 1.0 / left[pivot][pivot]
        left[pivot] = [entry * factor for entry in left[pivot]]
        right[pivot] = [entry * factor for entry in right[pivot]]
        for row in range(order):
            if row != pivot:
                scale = left[row][pivot]
                left[row] = [a - scale * b for a, b in zip(left[row], left[pivot])]
                right[row] = [a - scale * b for a, b in zip(right[row], right[pivot])]
    return right


def horner(coefficients, value):
    total = coefficients[-1] * value + coefficients[-2]
    for entry in coefficients[-3::-1]:
        total = total * value + entry
    return total


def tile_at(step, mine):
    high = lax.rem(mine // 2 + 1 - step // 2, 2)
    low = lax.rem(lax.rem(mine, 2) + (step + 1) // 2, 2)
    return 2 * high + low


def combine(factors, terms):
    total = terms[0] * factors[0]
    for factor, term in zip(factors[1:], terms[1:]):
        total = total + factor * term
    return total


def tree(terms):
    while len(terms) > 1:
        terms = [sum(terms[at : at + 2]) if at + 1 < len(terms) else terms[at] for at in range(0, len(terms), 2)]
    return terms[0]


def kernel(
    n,
    volts_hbm,
    num_hbm,
    weight_hbm,
    flags_hbm,
    positions_hbm,
    directions_hbm,
    pointing_hbm,
    power_ref,
    gains_ref,
    num_ref,
    weight_ref,
    flags_ref,
    positions_ref,
    directions_ref,
    pointing_ref,
    volts,
    message,
    gathered,
    outbox,
    inbox,
    ordered,
    products,
    phasors_0,
    phasors_1,
    phasors_2,
    phasors_3,
    ready,
    columns,
    table,
    local_ref,
    dual_ref,
    load_sem,
    cal_send,
    cal_recv,
    fit_send,
    fit_recv,
    out_send,
    out_recv,
    own_sem,
):
    me = lax.axis_index("chan")
    stations = flags_ref.shape[1]
    blocks = stations // LANES
    phasors = (phasors_0, phasors_1, phasors_2, phasors_3)
    tiles = len(phasors)
    width = phasors_0.shape[1]
    samples = volts.shape[1]
    half = samples // 2
    per_device = ready.shape[0] // n
    per_tile = n // tiles
    share = lax.rem(me, blocks)

    loads = [
        pltpu.make_async_copy(source, target, load_sem.at[index])
        for index, (source, target) in enumerate(
            (
                (num_hbm.at[0], num_ref),
                (weight_hbm.at[0], weight_ref),
                (flags_hbm, flags_ref),
                (positions_hbm, positions_ref),
                (directions_hbm, directions_ref),
                (pointing_hbm, pointing_ref),
                (volts_hbm.at[0], volts),
            )
        )
    ]
    for load in loads:
        load.start()

    barrier = pltpu.get_barrier_semaphore()

    @pl.loop(1, n)
    def _(offset):
        pl.semaphore_signal(
            barrier,
            inc=1,
            device_id={"chan": lax.rem(me + offset, n)},
            device_id_type=pl.DeviceIdType.MESH,
        )

    for load in loads[:3]:
        load.wait()
    for block in range(blocks):
        lanes = pl.ds(block * LANES, LANES)
        mask = flags_ref[:, lanes].astype(jnp.float32)
        message[block, 0:4, :] = mask * num_ref[:, lanes]
        for row in range(4):
            message[block, pl.ds(4 + row, 1), :] = mask * weight_ref[pl.ds(row // 2, 1), lanes]
    gathered[me] = message[share]

    pl.semaphore_wait(barrier, n - 1)

    def cal_copy(block, slot, peer, sent, received):
        return pltpu.make_async_remote_copy(
            src_ref=message.at[block],
            dst_ref=gathered.at[slot],
            send_sem=cal_send.at[sent],
            recv_sem=cal_recv.at[received],
            device_id={"chan": peer},
            device_id_type=pl.DeviceIdType.MESH,
        )

    @pl.loop(1, n)
    def _(offset):
        peer = lax.rem(me + offset, n)
        cal_copy(lax.rem(peer, blocks), me, peer, peer, me).start()

    for load in loads[3:6]:
        load.wait()
    for axis in range(2):
        for block in range(blocks):
            lanes = pl.ds(block * LANES, LANES)
            row = jnp.broadcast_to(positions_ref[pl.ds(axis, 1), lanes], (LANES, LANES))
            columns[axis, lanes, :] = row.T

    rest = directions_ref[...]
    table[...] = jnp.zeros_like(table)
    for term in range(3):
        head = rest.astype(jnp.bfloat16).astype(jnp.float32)
        table[pl.ds(8 * term, 2), :] = head
        rest = rest - head
    ratio = 1.0 + 0.15 * (2.0 * (me.astype(jnp.float32) + 0.5) / n)
    entries = directions_ref.shape[1]
    chunk = 64

    def make_phasors(step, straight):
        target = phasors[step]
        wanted = pointing_ref[tile_at(step, me // per_tile)]
        numbers = lax.broadcasted_iota(jnp.int32, (entries, width), 0)
        chosen = jnp.where(numbers == wanted, 1.0, 0.0).astype(jnp.bfloat16)
        terms = table[...].astype(jnp.bfloat16)
        found = jnp.dot(terms, chosen, preferred_element_type=jnp.float32)
        pointed = (found[0:8] + found[8:16] + found[16:24]) * ratio
        east = pointed[0:1]
        north = pointed[1:2]

        def one_chunk(part):
            start = part * chunk if straight else pl.multiple_of(part * chunk, chunk)
            rows = pl.ds(start, chunk)
            below = pl.ds(stations + start, chunk)
            for piece in range(width // LANES):
                lanes = pl.ds(piece * LANES, LANES)
                cut = slice(piece * LANES, (piece + 1) * LANES)
                turns = columns[0, rows, :] * east[:, cut] + columns[1, rows, :] * north[:, cut]
                turns = turns - ((turns + ROUNDING) - ROUNDING)
                square = turns * turns
                sine = horner(SINE, square) * turns
                cosine = horner(COSINE, square)
                target[rows, lanes] = (1.0 - sine * sine).astype(jnp.bfloat16)
                target[below, lanes] = (sine * cosine).astype(jnp.bfloat16)

        if straight:
            for part in range(stations // chunk):
                one_chunk(part)
        else:
            pl.loop(0, stations // chunk)(one_chunk)

    make_phasors(0, False)
    make_phasors(1, False)

    @pl.loop(1, n)
    def _(offset):
        peer = lax.rem(me + offset, n)
        cal_copy(0, peer, peer, peer, peer).wait_recv()

    pairs = n // 2
    basis = [basis_at(2.0 * (n - pair - 0.5) / n - 1.0) for pair in range(pairs)]
    sign = jnp.where(lax.broadcasted_iota(jnp.int32, (8, LANES), 0) < 4, 1.0, -1.0)
    solve_rows = []
    for pair in range(pairs):
        first = gathered[n - 1 - pair]
        second = gathered[pair]
        weight = jnp.concatenate([first[4:8], second[4:8]], axis=0)
        usable = jnp.where(weight > 0.0, 1.0, 0.0)
        damping = 1.0 / (weight + PENALTY)
        target = jnp.concatenate([first[0:4], second[0:4]], axis=0) * damping
        solve_rows.append((usable, PENALTY * damping, target))

    def both(term, value):
        value = value * sign if term % 2 else value
        return value + pltpu.roll(value, 4, 0)

    gram = [[None] * ORDER for _ in range(ORDER)]
    for first in range(ORDER):
        for second in range(first, ORDER):
            terms = [
                (basis[pair][first] * basis[pair][second]) * solve_rows[pair][0]
                for pair in range(pairs)
            ]
            gram[first][second] = both(first + second, tree(terms))
            gram[second][first] = gram[first][second]
        gram[first][first] = gram[first][first] + RIDGE
    inverse = invert_small(gram)
    local_ref[...] = jnp.zeros_like(local_ref)
    dual_ref[...] = jnp.zeros_like(dual_ref)
    nothing = jnp.zeros((8, LANES), jnp.float32)

    def sweep(_, line):
        signed = [entry * sign if term % 2 else entry for term, entry in enumerate(line)]
        numerator = [[] for _ in range(ORDER)]
        for pair in range(pairs):
            values = basis[pair]
            usable, damping, target = solve_rows[pair]
            fitted = tree([signed[0]] + [values[term] * signed[term] for term in range(1, ORDER)])
            dual = dual_ref[pair] + usable * (local_ref[pair] - fitted)
            local = target + damping * (fitted - dual)
            local_ref[pair] = local
            dual_ref[pair] = dual
            summand = usable * (local + dual)
            for term in range(ORDER):
                numerator[term].append(values[term] * summand if term else summand)
        sums = [both(term, tree(terms)) for term, terms in enumerate(numerator)]
        return tuple(
            tree([entry * total for entry, total in zip(inverse[first], sums)])
            for first in range(ORDER)
        )

    line = lax.fori_loop(0, ITERS, sweep, (nothing,) * ORDER)
    line = [entry[0:4] for entry in line]

    def fitted_at(channel):
        return combine(basis_at(2.0 * (channel.astype(jnp.float32) + 0.5) / n - 1.0), line)

    def fit_copy(source, slot, peer, sent, received):
        return pltpu.make_async_remote_copy(
            src_ref=outbox.at[source],
            dst_ref=inbox.at[slot],
            send_sem=fit_send.at[sent],
            recv_sem=fit_recv.at[received],
            device_id={"chan": peer},
            device_id_type=pl.DeviceIdType.MESH,
        )

    for offset in range(1, blocks):
        mate = lax.rem(share + offset, blocks)
        peer = me - share + mate
        outbox[mate] = fitted_at(peer)
        fit_copy(mate, share, peer, mate, share).start()
    inbox[share] = fitted_at(me)

    loads[6].wait()
    row = lax.broadcasted_iota(jnp.int32, (samples, samples), 0)
    col = lax.broadcasted_iota(jnp.int32, (samples, samples), 1)
    origin = jnp.where(row < half, 2 * row, 2 * (row - half) + 1)
    shuffle = jnp.where(col == origin, 1.0, 0.0).astype(jnp.bfloat16)
    for polar in range(2):
        ordered[polar] = jnp.dot(shuffle, volts[polar], preferred_element_type=jnp.float32)

    for offset in range(1, blocks):
        mate = lax.rem(share + offset, blocks)
        fit_copy(mate, mate, me - share + mate, mate, mate).wait_recv()
    for block in range(blocks):
        gains_ref[0, :, pl.ds(block * LANES, LANES)] = inbox[block]

    scale = flags_ref[...].astype(jnp.float32) * stations ** (-0.5)
    strip = 64
    for polar in range(2):
        gain_re = gains_ref[0, pl.ds(2 * polar, 1), :] * scale
        gain_im = gains_ref[0, pl.ds(2 * polar + 1, 1), :] * scale

        @pl.loop(0, samples // strip)
        def _(step):
            rows = pl.ds(pl.multiple_of(step * strip, strip), strip)
            real = ordered[polar, rows, :stations]
            imag = ordered[polar, rows, stations:]
            new_re = (gain_re * real + gain_im * imag).astype(jnp.bfloat16)
            new_im = (gain_re * imag - gain_im * real).astype(jnp.bfloat16)
            upper = pl.ds(pl.multiple_of(2 * polar * samples + step * strip, strip), strip)
            lower = pl.ds(pl.multiple_of((2 * polar + 1) * samples + step * strip, strip), strip)
            products[upper, :stations] = new_re
            products[upper, stations:] = new_im
            products[lower, :stations] = new_im
            products[lower, stations:] = -new_re

    def out_copy(owner, source, sent, received):
        rows = pl.ds(pl.multiple_of(owner * per_device, per_device), per_device)
        return pltpu.make_async_remote_copy(
            src_ref=ready.at[rows, :],
            dst_ref=power_ref.at[source],
            send_sem=out_send.at[sent],
            recv_sem=out_recv.at[received],
            device_id={"chan": owner},
            device_id_type=pl.DeviceIdType.MESH,
        )

    def own_copy():
        rows = pl.ds(pl.multiple_of(me * per_device, per_device), per_device)
        return pltpu.make_async_copy(ready.at[rows, :], power_ref.at[me], own_sem)

    for step in range(tiles):
        tile = tile_at(step, me // per_tile)
        beams = jnp.dot(products[...], phasors[step][...], preferred_element_type=jnp.float32)
        if 1 <= step < tiles - 1:
            make_phasors(step + 1, True)
        total = beams[:samples] * beams[:samples]
        for part in range(1, 4):
            piece = beams[part * samples : (part + 1) * samples]
            total = total + piece * piece
        mean = (total[:half] + total[half:]) * 0.5
        rows = pl.ds(pl.multiple_of(tile * width, width), width)
        ready[rows, :] = mean.T.astype(jnp.bfloat16)

        @pl.loop(0, per_tile)
        def _(index):
            owner = tile * per_tile + index
            if step < tiles - 1:
                out_copy(owner, me, owner, me).start()
            else:

                @pl.when(owner != me)
                def _():
                    out_copy(owner, me, owner, me).start()

                @pl.when(owner == me)
                def _():
                    own_copy().start()

    own_copy().wait()
    for offset in range(1, blocks):
        mate = lax.rem(share + offset, blocks)
        fit_copy(mate, share, me - share + mate, mate, share).wait_send()

    @pl.loop(1, n)
    def _(offset):
        peer = lax.rem(me + offset, n)
        cal_copy(lax.rem(peer, blocks), me, peer, peer, me).wait_send()
        out_copy(peer, me, peer, me).wait_send()
        out_copy(peer, peer, peer, peer).wait_recv()


def body(voltages, cal_num, cal_weight, flags, positions, directions, pointing):
    n = lax.axis_size("chan")
    count, polars, samples, depth = voltages.shape
    stations = flags.shape[1]
    blocks = stations // LANES
    assert count == 1 and polars == 2 and n % blocks == 0 and n % 4 == 0
    beams = pointing.shape[0]
    tiles = 4
    width = beams // tiles
    half = samples // 2
    entries = directions.shape[1]
    vmem = pl.BlockSpec(memory_space=pltpu.VMEM)
    hbm = pl.BlockSpec(memory_space=pltpu.HBM)
    f32 = jnp.float32
    power, gains = pl.pallas_call(
        functools.partial(kernel, n),
        out_shape=(
            pltpu.VMEM((n, beams // n, half), jnp.bfloat16),
            jax.ShapeDtypeStruct(cal_num.shape, f32),
        ),
        in_specs=[hbm] * 7,
        out_specs=(vmem, vmem),
        scratch_shapes=[
            pltpu.VMEM(cal_num.shape[1:], f32),
            pltpu.VMEM(cal_weight.shape[1:], f32),
            pltpu.VMEM(flags.shape, jnp.int32),
            pltpu.VMEM(positions.shape, f32),
            pltpu.VMEM(directions.shape, f32),
            pltpu.VMEM((tiles, 1, width), jnp.int32),
            pltpu.VMEM((polars, samples, depth), jnp.bfloat16),
            pltpu.VMEM((blocks, 8, LANES), f32),
            pltpu.VMEM((n, 8, LANES), f32),
            pltpu.VMEM((blocks, 4, LANES), f32),
            pltpu.VMEM((blocks, 4, LANES), f32),
            pltpu.VMEM((polars, samples, depth), f32),
            pltpu.VMEM((4 * samples, depth), jnp.bfloat16),
            *(pltpu.VMEM((depth, width), jnp.bfloat16) for _ in range(tiles)),
            pltpu.VMEM((beams, half), jnp.bfloat16),
            pltpu.VMEM((2, stations, LANES), f32),
            pltpu.VMEM((32, entries), f32),
            pltpu.VMEM((n // 2, 8, LANES), f32),
            pltpu.VMEM((n // 2, 8, LANES), f32),
            pltpu.SemaphoreType.DMA((7,)),
            pltpu.SemaphoreType.DMA((n,)),
            pltpu.SemaphoreType.DMA((n,)),
            pltpu.SemaphoreType.DMA((blocks,)),
            pltpu.SemaphoreType.DMA((blocks,)),
            pltpu.SemaphoreType.DMA((n,)),
            pltpu.SemaphoreType.DMA((n,)),
            pltpu.SemaphoreType.DMA,
        ],
        compiler_params=pltpu.CompilerParams(
            collective_id=0, has_side_effects=True, vmem_limit_bytes=40 * 2**20
        ),
    )(
        *(
            pltpu.with_memory_space_constraint(operand, pltpu.HBM)
            for operand in (
                voltages,
                cal_num,
                cal_weight,
                flags,
                positions,
                directions,
                pointing.reshape(tiles, 1, width),
            )
        )
    )
    return jnp.transpose(power, (1, 0, 2)), gains


def solution(mesh):
    return jax.shard_map(
        body,
        mesh=mesh,
        in_specs=(
            P(("group", "chan"), None, None, None),
            P(("group", "chan"), None, None),
            P(("group", "chan"), None, None),
            P(("group", "chan"), None),
            P(),
            P(),
            P("group"),
        ),
        out_specs=(P(("group", "chan"), None, None), P(("group", "chan"), None, None)),
        check_vma=False,
    )
```

```python
import functools
import jax
import jax.numpy as jnp
from jax import lax
from jax.experimental import pallas as pl
from jax.experimental.pallas import tpu as pltpu
from jax.sharding import PartitionSpec as P

ITERS = 8
PENALTY = 2.0
RIDGE = 1.0
ORDER = 4
LANES = 128
ROUNDING = 1.5 * 2.0**23
SINE = (4.44288292, -7.30824569, 3.60635422, -0.84611165, 0.10982452)
COSINE = (1.4142135, -6.97885095, 5.73946038, -1.88355791, 0.31068803)


def basis_at(place):
    return (
        1.0,
        place,
        0.5 * (3.0 * place * place - 1.0),
        0.5 * (5.0 * place * place * place - 3.0 * place),
    )


def invert_small(matrix):
    order = len(matrix)
    unit = jnp.ones_like(matrix[0][0])
    nothing = jnp.zeros_like(unit)
    left = [list(line) for line in matrix]
    right = [[unit if row == col else nothing for col in range(order)] for row in range(order)]
    for pivot in range(order):
        factor = 1.0 / left[pivot][pivot]
        left[pivot] = [entry * factor for entry in left[pivot]]
        right[pivot] = [entry * factor for entry in right[pivot]]
        for row in range(order):
            if row != pivot:
                scale = left[row][pivot]
                left[row] = [a - scale * b for a, b in zip(left[row], left[pivot])]
                right[row] = [a - scale * b for a, b in zip(right[row], right[pivot])]
    return right


def horner(coefficients, value):
    total = coefficients[-1] * value + coefficients[-2]
    for entry in coefficients[-3::-1]:
        total = total * value + entry
    return total


def tile_at(step, mine, tiles):
    if tiles == 4:
        high = lax.rem(mine // 2 + 1 - step // 2, 2)
        low = lax.rem(lax.rem(mine, 2) + (step + 1) // 2, 2)
        return 2 * high + low
    return lax.rem(mine + tiles // 2 + step, tiles)


def combine(factors, terms):
    total = terms[0] * factors[0]
    for factor, term in zip(factors[1:], terms[1:]):
        total = total + factor * term
    return total


def tree(terms):
    while len(terms) > 1:
        terms = [sum(terms[at : at + 2]) if at + 1 < len(terms) else terms[at] for at in range(0, len(terms), 2)]
    return terms[0]


def kernel(
    n,
    tiles,
    volts_hbm,
    num_hbm,
    weight_hbm,
    flags_hbm,
    positions_hbm,
    directions_hbm,
    pointing_hbm,
    power_ref,
    gains_ref,
    num_ref,
    weight_ref,
    flags_ref,
    positions_ref,
    directions_ref,
    pointing_ref,
    volts,
    message,
    gathered,
    outbox,
    inbox,
    summed,
    products,
    phasors,
    ready,
    columns,
    table,
    local_ref,
    dual_ref,
    load_sem,
    cal_send,
    cal_recv,
    fit_send,
    fit_recv,
    out_send,
    out_recv,
    own_sem,
):
    me = lax.axis_index("chan")
    stations = flags_ref.shape[1]
    blocks = stations // LANES
    width = phasors.shape[2]
    samples = volts.shape[1]
    half = samples // 2
    per_device = ready.shape[0] // n
    per_tile = n // tiles
    share = lax.rem(me, blocks)

    loads = [
        pltpu.make_async_copy(source, target, load_sem.at[index])
        for index, (source, target) in enumerate(
            (
                (num_hbm.at[0], num_ref),
                (weight_hbm.at[0], weight_ref),
                (flags_hbm, flags_ref),
                (positions_hbm, positions_ref),
                (directions_hbm, directions_ref),
                (pointing_hbm, pointing_ref),
                (volts_hbm.at[0], volts),
            )
        )
    ]
    for load in loads:
        load.start()

    barrier = pltpu.get_barrier_semaphore()

    @pl.loop(1, n)
    def _(offset):
        pl.semaphore_signal(
            barrier,
            inc=1,
            device_id={"chan": lax.rem(me + offset, n)},
            device_id_type=pl.DeviceIdType.MESH,
        )

    for load in loads[:3]:
        load.wait()
    for block in range(blocks):
        lanes = pl.ds(block * LANES, LANES)
        mask = flags_ref[:, lanes].astype(jnp.float32)
        message[block, 0:4, :] = mask * num_ref[:, lanes]
        for row in range(4):
            message[block, pl.ds(4 + row, 1), :] = mask * weight_ref[pl.ds(row // 2, 1), lanes]
    gathered[me] = message[share]

    pl.semaphore_wait(barrier, n - 1)

    def cal_copy(block, slot, peer, sent, received):
        return pltpu.make_async_remote_copy(
            src_ref=message.at[block],
            dst_ref=gathered.at[slot],
            send_sem=cal_send.at[sent],
            recv_sem=cal_recv.at[received],
            device_id={"chan": peer},
            device_id_type=pl.DeviceIdType.MESH,
        )

    @pl.loop(1, n)
    def _(offset):
        peer = lax.rem(me + offset, n)
        cal_copy(lax.rem(peer, blocks), me, peer, peer, me).start()

    for load in loads[3:6]:
        load.wait()
    for axis in range(2):
        for block in range(blocks):
            lanes = pl.ds(block * LANES, LANES)
            row = jnp.broadcast_to(positions_ref[pl.ds(axis, 1), lanes], (LANES, LANES))
            columns[axis, lanes, :] = row.T

    entries = directions_ref.shape[1]
    span = table.shape[2]
    rest = directions_ref[...]
    table[...] = jnp.zeros_like(table)
    for term in range(3):
        head = rest.astype(jnp.bfloat16).astype(jnp.float32)
        for part in range(entries // span):
            table[part, pl.ds(8 * term, 2), :] = head[:, part * span : (part + 1) * span]
        rest = rest - head
    ratio = 1.0 + 0.15 * (2.0 * (me.astype(jnp.float32) + 0.5) / n)
    chunk = 64

    def make_phasors(step):
        wanted = pointing_ref[tile_at(step, me // per_tile, tiles)]
        numbers = lax.broadcasted_iota(jnp.int32, (span, width), 0)

        def search(part, found):
            chosen = jnp.where(numbers == wanted - part * span, 1.0, 0.0).astype(jnp.bfloat16)
            terms = table[part].astype(jnp.bfloat16)
            return found + jnp.dot(terms, chosen, preferred_element_type=jnp.float32)

        nowhere = jnp.zeros((table.shape[1], width), jnp.float32)
        found = lax.fori_loop(0, entries // span, search, nowhere)
        pointed = (found[0:8] + found[8:16] + found[16:24]) * ratio
        east = pointed[0:1]
        north = pointed[1:2]

        @pl.loop(0, stations // chunk)
        def _(part):
            rows = pl.ds(pl.multiple_of(part * chunk, chunk), chunk)
            below = pl.ds(pl.multiple_of(stations + part * chunk, chunk), chunk)
            for piece in range(width // LANES):
                lanes = pl.ds(piece * LANES, LANES)
                cut = slice(piece * LANES, (piece + 1) * LANES)
                turns = columns[0, rows, :] * east[:, cut] + columns[1, rows, :] * north[:, cut]
                turns = turns - ((turns + ROUNDING) - ROUNDING)
                square = turns * turns
                sine = horner(SINE, square) * turns
                cosine = horner(COSINE, square)
                phasors[step, rows, lanes] = (1.0 - sine * sine).astype(jnp.bfloat16)
                phasors[step, below, lanes] = (sine * cosine).astype(jnp.bfloat16)

    make_phasors(0)

    @pl.loop(1, n)
    def _(offset):
        peer = lax.rem(me + offset, n)
        cal_copy(0, peer, peer, peer, peer).wait_recv()

    pairs = n // 2
    basis = [basis_at(2.0 * (n - pair - 0.5) / n - 1.0) for pair in range(pairs)]
    sign = jnp.where(lax.broadcasted_iota(jnp.int32, (8, LANES), 0) < 4, 1.0, -1.0)
    solve_rows = []
    for pair in range(pairs):
        first = gathered[n - 1 - pair]
        second = gathered[pair]
        weight = jnp.concatenate([first[4:8], second[4:8]], axis=0)
        usable = jnp.where(weight > 0.0, 1.0, 0.0)
        damping = 1.0 / (weight + PENALTY)
        target = jnp.concatenate([first[0:4], second[0:4]], axis=0) * damping
        solve_rows.append((usable, PENALTY * damping, target))

    def both(term, value):
        value = value * sign if term % 2 else value
        return value + pltpu.roll(value, 4, 0)

    gram = [[None] * ORDER for _ in range(ORDER)]
    for first in range(ORDER):
        for second in range(first, ORDER):
            terms = [
                (basis[pair][first] * basis[pair][second]) * solve_rows[pair][0]
                for pair in range(pairs)
            ]
            gram[first][second] = both(first + second, tree(terms))
            gram[second][first] = gram[first][second]
        gram[first][first] = gram[first][first] + RIDGE
    inverse = invert_small(gram)
    local_ref[...] = jnp.zeros_like(local_ref)
    dual_ref[...] = jnp.zeros_like(dual_ref)
    nothing = jnp.zeros((8, LANES), jnp.float32)

    def sweep(_, line):
        signed = [entry * sign if term % 2 else entry for term, entry in enumerate(line)]
        numerator = [[] for _ in range(ORDER)]
        for pair in range(pairs):
            values = basis[pair]
            usable, damping, target = solve_rows[pair]
            fitted = tree([signed[0]] + [values[term] * signed[term] for term in range(1, ORDER)])
            dual = dual_ref[pair] + usable * (local_ref[pair] - fitted)
            local = target + damping * (fitted - dual)
            local_ref[pair] = local
            dual_ref[pair] = dual
            summand = usable * (local + dual)
            for term in range(ORDER):
                numerator[term].append(values[term] * summand if term else summand)
        sums = [both(term, tree(terms)) for term, terms in enumerate(numerator)]
        return tuple(
            tree([entry * total for entry, total in zip(inverse[first], sums)])
            for first in range(ORDER)
        )

    line = lax.fori_loop(0, ITERS, sweep, (nothing,) * ORDER)
    line = [entry[0:4] for entry in line]

    def fitted_at(channel):
        return combine(basis_at(2.0 * (channel.astype(jnp.float32) + 0.5) / n - 1.0), line)

    def fit_copy(source, slot, peer, sent, received):
        return pltpu.make_async_remote_copy(
            src_ref=outbox.at[source],
            dst_ref=inbox.at[slot],
            send_sem=fit_send.at[sent],
            recv_sem=fit_recv.at[received],
            device_id={"chan": peer},
            device_id_type=pl.DeviceIdType.MESH,
        )

    for offset in range(1, blocks):
        mate = lax.rem(share + offset, blocks)
        peer = me - share + mate
        outbox[mate] = fitted_at(peer)
        fit_copy(mate, share, peer, mate, share).start()
    inbox[share] = fitted_at(me)

    loads[6].wait()
    ahead = 1
    for offset in range(1, blocks):
        mate = lax.rem(share + offset, blocks)
        fit_copy(mate, mate, me - share + mate, mate, mate).wait_recv()
    for block in range(blocks):
        gains_ref[0, :, pl.ds(block * LANES, LANES)] = inbox[block]

    scale = flags_ref[...].astype(jnp.float32) * stations ** (-0.5)
    strip = 32
    for polar in range(2):
        gain_re = gains_ref[0, pl.ds(2 * polar, 1), :] * scale
        gain_im = gains_ref[0, pl.ds(2 * polar + 1, 1), :] * scale

        @pl.loop(0, samples // strip)
        def _(step):
            rows = pl.ds(pl.multiple_of(step * strip, strip), strip)
            real = volts[polar, rows, :stations].astype(jnp.float32)
            imag = volts[polar, rows, stations:].astype(jnp.float32)
            new_re = (gain_re * real + gain_im * imag).astype(jnp.bfloat16)
            new_im = (gain_re * imag - gain_im * real).astype(jnp.bfloat16)
            upper = pl.ds(pl.multiple_of(2 * polar * samples + step * strip, strip), strip)
            lower = pl.ds(pl.multiple_of((2 * polar + 1) * samples + step * strip, strip), strip)
            products[upper, :stations] = new_re
            products[upper, stations:] = new_im
            products[lower, :stations] = new_im
            products[lower, stations:] = -new_re

    def out_copy(owner, source, sent, received):
        rows = pl.ds(pl.multiple_of(owner * per_device, per_device), per_device)
        return pltpu.make_async_remote_copy(
            src_ref=ready.at[rows, :],
            dst_ref=power_ref.at[source],
            send_sem=out_send.at[sent],
            recv_sem=out_recv.at[received],
            device_id={"chan": owner},
            device_id_type=pl.DeviceIdType.MESH,
        )

    def own_copy():
        rows = pl.ds(pl.multiple_of(me * per_device, per_device), per_device)
        return pltpu.make_async_copy(ready.at[rows, :], power_ref.at[me], own_sem)

    @pl.loop(0, tiles)
    def _(step):
        tile = tile_at(step, me // per_tile, tiles)
        summed[...] = jnp.zeros_like(summed)

        @pl.loop(0, 2)
        def _(polar):
            at = pl.ds(pl.multiple_of(2 * polar * samples, samples), 2 * samples)
            beams = jnp.dot(products[at, :], phasors[step], preferred_element_type=jnp.float32)
            total = beams[:samples] * beams[:samples] + beams[samples:] * beams[samples:]
            for piece in range(width // LANES):
                summed[piece] += total[:, piece * LANES : (piece + 1) * LANES]

        for piece in range(width // LANES):
            even = summed[piece, pl.ds(0, half, stride=2), :]
            odd = summed[piece, pl.ds(1, half, stride=2), :]
            rows = pl.ds(pl.multiple_of(tile * width + piece * LANES, LANES), LANES)
            ready[rows, :] = ((even + odd) * 0.5).T.astype(jnp.bfloat16)

        @pl.loop(0, per_tile)
        def _(index):
            owner = tile * per_tile + index

            @pl.when(owner != me)
            def _():
                out_copy(owner, me, owner, me).start()

            @pl.when(owner == me)
            def _():
                own_copy().start()

        @pl.when(step < tiles - ahead)
        def _():
            make_phasors(step + ahead)

    own_copy().wait()
    for offset in range(1, blocks):
        mate = lax.rem(share + offset, blocks)
        fit_copy(mate, share, me - share + mate, mate, share).wait_send()

    @pl.loop(1, n)
    def _(offset):
        peer = lax.rem(me + offset, n)
        cal_copy(lax.rem(peer, blocks), me, peer, peer, me).wait_send()
        out_copy(peer, me, peer, me).wait_send()
        out_copy(peer, peer, peer, peer).wait_recv()


def body(voltages, cal_num, cal_weight, flags, positions, directions, pointing):
    n = lax.axis_size("chan")
    count, polars, samples, depth = voltages.shape
    stations = flags.shape[1]
    blocks = stations // LANES
    assert count == 1 and polars == 2 and n % blocks == 0 and n % 2 == 0
    beams = pointing.shape[0]
    tiles = 4
    width = beams // tiles
    half = samples // 2
    entries = directions.shape[1]
    vmem = pl.BlockSpec(memory_space=pltpu.VMEM)
    hbm = pl.BlockSpec(memory_space=pltpu.HBM)
    f32 = jnp.float32
    power, gains = pl.pallas_call(
        functools.partial(kernel, n, tiles),
        out_shape=(
            pltpu.VMEM((n, beams // n, half), jnp.bfloat16),
            jax.ShapeDtypeStruct(cal_num.shape, f32),
        ),
        in_specs=[hbm] * 7,
        out_specs=(vmem, vmem),
        scratch_shapes=[
            pltpu.VMEM(cal_num.shape[1:], f32),
            pltpu.VMEM(cal_weight.shape[1:], f32),
            pltpu.VMEM(flags.shape, jnp.int32),
            pltpu.VMEM(positions.shape, f32),
            pltpu.VMEM(directions.shape, f32),
            pltpu.VMEM((tiles, 1, width), jnp.int32),
            pltpu.VMEM((polars, samples, depth), jnp.bfloat16),
            pltpu.VMEM((blocks, 8, LANES), f32),
            pltpu.VMEM((n, 8, LANES), f32),
            pltpu.VMEM((blocks, 4, LANES), f32),
            pltpu.VMEM((blocks, 4, LANES), f32),
            pltpu.VMEM((width // LANES, samples, LANES), f32),
            pltpu.VMEM((4 * samples, depth), jnp.bfloat16),
            pltpu.VMEM((tiles, depth, width), jnp.bfloat16),
            pltpu.VMEM((beams, half), jnp.bfloat16),
            pltpu.VMEM((2, stations, LANES), f32),
            pltpu.VMEM((entries // 256, 32, 256), f32),
            pltpu.VMEM((n // 2, 8, LANES), f32),
            pltpu.VMEM((n // 2, 8, LANES), f32),
            pltpu.SemaphoreType.DMA((7,)),
            pltpu.SemaphoreType.DMA((n,)),
            pltpu.SemaphoreType.DMA((n,)),
            pltpu.SemaphoreType.DMA((blocks,)),
            pltpu.SemaphoreType.DMA((blocks,)),
            pltpu.SemaphoreType.DMA((n,)),
            pltpu.SemaphoreType.DMA((n,)),
            pltpu.SemaphoreType.DMA,
        ],
        compiler_params=pltpu.CompilerParams(
            collective_id=0, has_side_effects=True, vmem_limit_bytes=40 * 2**20
        ),
    )(
        *(
            pltpu.with_memory_space_constraint(operand, pltpu.HBM)
            for operand in (
                voltages,
                cal_num,
                cal_weight,
                flags,
                positions,
                directions,
                pointing.reshape(tiles, 1, width),
            )
        )
    )
    return jnp.transpose(power, (1, 0, 2)), gains


def solution(mesh):
    return jax.shard_map(
        body,
        mesh=mesh,
        in_specs=(
            P(("group", "chan"), None, None, None),
            P(("group", "chan"), None, None),
            P(("group", "chan"), None, None),
            P(("group", "chan"), None),
            P(),
            P(),
            P("group"),
        ),
        out_specs=(P(("group", "chan"), None, None), P(("group", "chan"), None, None)),
        check_vma=False,
    )
```

```python
import functools
import jax
import jax.numpy as jnp
from jax import lax
from jax.experimental import pallas as pl
from jax.experimental.pallas import tpu as pltpu
from jax.sharding import PartitionSpec as P

ITERS = 8
PENALTY = 2.0
RIDGE = 1.0
ORDER = 4
LANES = 128
ROUNDING = 1.5 * 2.0**23
SINE = (4.44288292, -7.30824569, 3.60635422, -0.84611165, 0.10982452)
COSINE = (1.4142135, -6.97885095, 5.73946038, -1.88355791, 0.31068803)


def basis_at(place):
    return (
        1.0,
        place,
        0.5 * (3.0 * place * place - 1.0),
        0.5 * (5.0 * place * place * place - 3.0 * place),
    )


def invert_small(matrix):
    order = len(matrix)
    unit = jnp.ones_like(matrix[0][0])
    nothing = jnp.zeros_like(unit)
    left = [list(line) for line in matrix]
    right = [[unit if row == col else nothing for col in range(order)] for row in range(order)]
    for pivot in range(order):
        factor = 1.0 / left[pivot][pivot]
        left[pivot] = [entry * factor for entry in left[pivot]]
        right[pivot] = [entry * factor for entry in right[pivot]]
        for row in range(order):
            if row != pivot:
                scale = left[row][pivot]
                left[row] = [a - scale * b for a, b in zip(left[row], left[pivot])]
                right[row] = [a - scale * b for a, b in zip(right[row], right[pivot])]
    return right


def horner(coefficients, value):
    total = coefficients[-1] * value + coefficients[-2]
    for entry in coefficients[-3::-1]:
        total = total * value + entry
    return total


def tile_at(step, mine, tiles):
    if tiles == 4:
        high = lax.rem(mine // 2 + 1 - step // 2, 2)
        low = lax.rem(lax.rem(mine, 2) + (step + 1) // 2, 2)
        return 2 * high + low
    return lax.rem(mine + tiles // 2 + step, tiles)


def combine(factors, terms):
    total = terms[0] * factors[0]
    for factor, term in zip(factors[1:], terms[1:]):
        total = total + factor * term
    return total


def tree(terms):
    while len(terms) > 1:
        terms = [sum(terms[at : at + 2]) if at + 1 < len(terms) else terms[at] for at in range(0, len(terms), 2)]
    return terms[0]


def kernel(
    n,
    tiles,
    volts_hbm,
    num_hbm,
    weight_hbm,
    flags_hbm,
    positions_hbm,
    directions_hbm,
    pointing_hbm,
    power_ref,
    gains_ref,
    num_ref,
    weight_ref,
    flags_ref,
    positions_ref,
    directions_ref,
    pointing_ref,
    volts,
    message,
    gathered,
    outbox,
    inbox,
    ordered,
    products,
    phasors,
    ready,
    columns,
    table,
    pointed,
    local_ref,
    dual_ref,
    load_sem,
    cal_send,
    cal_recv,
    fit_send,
    fit_recv,
    out_send,
    out_recv,
    own_sem,
):
    me = lax.axis_index("chan")
    stations = flags_ref.shape[1]
    blocks = stations // LANES
    width = phasors.shape[2]
    samples = volts.shape[1]
    half = samples // 2
    per_device = ready.shape[0] // n
    per_tile = n // tiles
    share = lax.rem(me, blocks)

    loads = [
        pltpu.make_async_copy(source, target, load_sem.at[index])
        for index, (source, target) in enumerate(
            (
                (num_hbm.at[0], num_ref),
                (weight_hbm.at[0], weight_ref),
                (flags_hbm, flags_ref),
                (positions_hbm, positions_ref),
                (directions_hbm, directions_ref),
                (pointing_hbm, pointing_ref),
                (volts_hbm.at[0], volts),
            )
        )
    ]
    for load in loads:
        load.start()

    barrier = pltpu.get_barrier_semaphore()

    @pl.loop(1, n)
    def _(offset):
        pl.semaphore_signal(
            barrier,
            inc=1,
            device_id={"chan": lax.rem(me + offset, n)},
            device_id_type=pl.DeviceIdType.MESH,
        )

    for load in loads[:3]:
        load.wait()
    for block in range(blocks):
        lanes = pl.ds(block * LANES, LANES)
        mask = flags_ref[:, lanes].astype(jnp.float32)
        message[block, 0:4, :] = mask * num_ref[:, lanes]
        for row in range(4):
            message[block, pl.ds(4 + row, 1), :] = mask * weight_ref[pl.ds(row // 2, 1), lanes]
    gathered[me] = message[share]

    pl.semaphore_wait(barrier, n - 1)

    def cal_copy(block, slot, peer, sent, received):
        return pltpu.make_async_remote_copy(
            src_ref=message.at[block],
            dst_ref=gathered.at[slot],
            send_sem=cal_send.at[sent],
            recv_sem=cal_recv.at[received],
            device_id={"chan": peer},
            device_id_type=pl.DeviceIdType.MESH,
        )

    @pl.loop(1, n)
    def _(offset):
        peer = lax.rem(me + offset, n)
        cal_copy(lax.rem(peer, blocks), me, peer, peer, me).start()

    for load in loads[3:6]:
        load.wait()
    for axis in range(2):
        for block in range(blocks):
            lanes = pl.ds(block * LANES, LANES)
            row = jnp.broadcast_to(positions_ref[pl.ds(axis, 1), lanes], (LANES, LANES))
            columns[axis, lanes, :] = row.T

    rest = directions_ref[...]
    table[...] = jnp.zeros_like(table)
    for term in range(3):
        head = rest.astype(jnp.bfloat16).astype(jnp.float32)
        table[pl.ds(8 * term, 2), :] = head
        rest = rest - head
    ratio = 1.0 + 0.15 * (2.0 * (me.astype(jnp.float32) + 0.5) / n)
    entries = directions_ref.shape[1]
    chunk = 32

    @pl.loop(0, tiles)
    def _(tile):
        numbers = lax.broadcasted_iota(jnp.int32, (entries, width), 0)
        chosen = jnp.where(numbers == pointing_ref[tile], 1.0, 0.0).astype(jnp.bfloat16)
        terms = table[...].astype(jnp.bfloat16)
        found = jnp.dot(terms, chosen, preferred_element_type=jnp.float32)
        pointed[tile] = (found[0:8] + found[8:16] + found[16:24]) * ratio

    def make_phasors(step):
        tile = tile_at(step, me // per_tile, tiles)
        east = pointed[tile, 0:1, :]
        north = pointed[tile, 1:2, :]

        @pl.loop(0, stations // chunk)
        def _(part):
            rows = pl.ds(pl.multiple_of(part * chunk, chunk), chunk)
            below = pl.ds(pl.multiple_of(stations + part * chunk, chunk), chunk)
            for piece in range(width // LANES):
                lanes = pl.ds(piece * LANES, LANES)
                cut = slice(piece * LANES, (piece + 1) * LANES)
                turns = columns[0, rows, :] * east[:, cut] + columns[1, rows, :] * north[:, cut]
                turns = turns - ((turns + ROUNDING) - ROUNDING)
                square = turns * turns
                sine = horner(SINE, square) * turns
                cosine = horner(COSINE, square)
                phasors[step, rows, lanes] = (1.0 - sine * sine).astype(jnp.bfloat16)
                phasors[step, below, lanes] = (sine * cosine).astype(jnp.bfloat16)

    make_phasors(0)

    @pl.loop(1, n)
    def _(offset):
        peer = lax.rem(me + offset, n)
        cal_copy(0, peer, peer, peer, peer).wait_recv()

    pairs = n // 2
    basis = [basis_at(2.0 * (n - pair - 0.5) / n - 1.0) for pair in range(pairs)]
    sign = jnp.where(lax.broadcasted_iota(jnp.int32, (8, LANES), 0) < 4, 1.0, -1.0)
    solve_rows = []
    for pair in range(pairs):
        first = gathered[n - 1 - pair]
        second = gathered[pair]
        weight = jnp.concatenate([first[4:8], second[4:8]], axis=0)
        usable = jnp.where(weight > 0.0, 1.0, 0.0)
        damping = 1.0 / (weight + PENALTY)
        target = jnp.concatenate([first[0:4], second[0:4]], axis=0) * damping
        solve_rows.append((usable, PENALTY * damping, target))

    def both(term, value):
        value = value * sign if term % 2 else value
        return value + pltpu.roll(value, 4, 0)

    gram = [[None] * ORDER for _ in range(ORDER)]
    for first in range(ORDER):
        for second in range(first, ORDER):
            terms = [
                (basis[pair][first] * basis[pair][second]) * solve_rows[pair][0]
                for pair in range(pairs)
            ]
            gram[first][second] = both(first + second, tree(terms))
            gram[second][first] = gram[first][second]
        gram[first][first] = gram[first][first] + RIDGE
    inverse = invert_small(gram)
    local_ref[...] = jnp.zeros_like(local_ref)
    dual_ref[...] = jnp.zeros_like(dual_ref)
    nothing = jnp.zeros((8, LANES), jnp.float32)

    def sweep(_, line):
        signed = [entry * sign if term % 2 else entry for term, entry in enumerate(line)]
        numerator = [[] for _ in range(ORDER)]
        for pair in range(pairs):
            values = basis[pair]
            usable, damping, target = solve_rows[pair]
            fitted = tree([signed[0]] + [values[term] * signed[term] for term in range(1, ORDER)])
            dual = dual_ref[pair] + usable * (local_ref[pair] - fitted)
            local = target + damping * (fitted - dual)
            local_ref[pair] = local
            dual_ref[pair] = dual
            summand = usable * (local + dual)
            for term in range(ORDER):
                numerator[term].append(values[term] * summand if term else summand)
        sums = [both(term, tree(terms)) for term, terms in enumerate(numerator)]
        return tuple(
            tree([entry * total for entry, total in zip(inverse[first], sums)])
            for first in range(ORDER)
        )

    line = lax.fori_loop(0, ITERS, sweep, (nothing,) * ORDER)
    line = [entry[0:4] for entry in line]

    def fitted_at(channel):
        return combine(basis_at(2.0 * (channel.astype(jnp.float32) + 0.5) / n - 1.0), line)

    def fit_copy(source, slot, peer, sent, received):
        return pltpu.make_async_remote_copy(
            src_ref=outbox.at[source],
            dst_ref=inbox.at[slot],
            send_sem=fit_send.at[sent],
            recv_sem=fit_recv.at[received],
            device_id={"chan": peer},
            device_id_type=pl.DeviceIdType.MESH,
        )

    for offset in range(1, blocks):
        mate = lax.rem(share + offset, blocks)
        peer = me - share + mate
        outbox[mate] = fitted_at(peer)
        fit_copy(mate, share, peer, mate, share).start()
    inbox[share] = fitted_at(me)

    loads[6].wait()
    row = lax.broadcasted_iota(jnp.int32, (samples, samples), 0)
    col = lax.broadcasted_iota(jnp.int32, (samples, samples), 1)
    origin = jnp.where(row < half, 2 * row, 2 * (row - half) + 1)
    shuffle = jnp.where(col == origin, 1.0, 0.0).astype(jnp.bfloat16)
    for polar in range(2):
        ordered[polar] = jnp.dot(shuffle, volts[polar], preferred_element_type=jnp.float32)

    make_phasors(1)
    for offset in range(1, blocks):
        mate = lax.rem(share + offset, blocks)
        fit_copy(mate, mate, me - share + mate, mate, mate).wait_recv()
    for block in range(blocks):
        gains_ref[0, :, pl.ds(block * LANES, LANES)] = inbox[block]

    scale = flags_ref[...].astype(jnp.float32) * stations ** (-0.5)
    strip = 64
    for polar in range(2):
        gain_re = gains_ref[0, pl.ds(2 * polar, 1), :] * scale
        gain_im = gains_ref[0, pl.ds(2 * polar + 1, 1), :] * scale

        @pl.loop(0, samples // strip)
        def _(step):
            rows = pl.ds(pl.multiple_of(step * strip, strip), strip)
            real = ordered[polar, rows, :stations]
            imag = ordered[polar, rows, stations:]
            new_re = (gain_re * real + gain_im * imag).astype(jnp.bfloat16)
            new_im = (gain_re * imag - gain_im * real).astype(jnp.bfloat16)
            upper = pl.ds(pl.multiple_of(2 * polar * samples + step * strip, strip), strip)
            lower = pl.ds(pl.multiple_of((2 * polar + 1) * samples + step * strip, strip), strip)
            products[upper, :stations] = new_re
            products[upper, stations:] = new_im
            products[lower, :stations] = new_im
            products[lower, stations:] = -new_re

    def out_copy(owner, source, sent, received):
        rows = pl.ds(pl.multiple_of(owner * per_device, per_device), per_device)
        return pltpu.make_async_remote_copy(
            src_ref=ready.at[rows, :],
            dst_ref=power_ref.at[source],
            send_sem=out_send.at[sent],
            recv_sem=out_recv.at[received],
            device_id={"chan": owner},
            device_id_type=pl.DeviceIdType.MESH,
        )

    def own_copy():
        rows = pl.ds(pl.multiple_of(me * per_device, per_device), per_device)
        return pltpu.make_async_copy(ready.at[rows, :], power_ref.at[me], own_sem)

    @pl.loop(0, tiles)
    def _(step):
        @pl.when(step >= 2)
        def _():
            make_phasors(step)

        tile = tile_at(step, me // per_tile, tiles)
        beams = jnp.dot(products[...], phasors[step], preferred_element_type=jnp.float32)
        total = beams[:samples] * beams[:samples]
        for part in range(1, 4):
            piece = beams[part * samples : (part + 1) * samples]
            total = total + piece * piece
        mean = (total[:half] + total[half:]) * 0.5
        rows = pl.ds(pl.multiple_of(tile * width, width), width)
        ready[rows, :] = mean.T.astype(jnp.bfloat16)

        @pl.loop(0, per_tile)
        def _(index):
            owner = tile * per_tile + index

            @pl.when(owner != me)
            def _():
                out_copy(owner, me, owner, me).start()

            @pl.when(owner == me)
            def _():
                own_copy().start()

    own_copy().wait()
    for offset in range(1, blocks):
        mate = lax.rem(share + offset, blocks)
        fit_copy(mate, share, me - share + mate, mate, share).wait_send()

    @pl.loop(1, n)
    def _(offset):
        peer = lax.rem(me + offset, n)
        cal_copy(lax.rem(peer, blocks), me, peer, peer, me).wait_send()
        out_copy(peer, me, peer, me).wait_send()
        out_copy(peer, peer, peer, peer).wait_recv()


def body(voltages, cal_num, cal_weight, flags, positions, directions, pointing):
    n = lax.axis_size("chan")
    count, polars, samples, depth = voltages.shape
    stations = flags.shape[1]
    blocks = stations // LANES
    assert count == 1 and polars == 2 and n % blocks == 0 and n % 2 == 0
    beams = pointing.shape[0]
    tiles = 4
    width = beams // tiles
    half = samples // 2
    entries = directions.shape[1]
    vmem = pl.BlockSpec(memory_space=pltpu.VMEM)
    hbm = pl.BlockSpec(memory_space=pltpu.HBM)
    f32 = jnp.float32
    power, gains = pl.pallas_call(
        functools.partial(kernel, n, tiles),
        out_shape=(
            pltpu.VMEM((n, beams // n, half), jnp.bfloat16),
            jax.ShapeDtypeStruct(cal_num.shape, f32),
        ),
        in_specs=[hbm] * 7,
        out_specs=(vmem, vmem),
        scratch_shapes=[
            pltpu.VMEM(cal_num.shape[1:], f32),
            pltpu.VMEM(cal_weight.shape[1:], f32),
            pltpu.VMEM(flags.shape, jnp.int32),
            pltpu.VMEM(positions.shape, f32),
            pltpu.VMEM(directions.shape, f32),
            pltpu.VMEM((tiles, 1, width), jnp.int32),
            pltpu.VMEM((polars, samples, depth), jnp.bfloat16),
            pltpu.VMEM((blocks, 8, LANES), f32),
            pltpu.VMEM((n, 8, LANES), f32),
            pltpu.VMEM((blocks, 4, LANES), f32),
            pltpu.VMEM((blocks, 4, LANES), f32),
            pltpu.VMEM((polars, samples, depth), f32),
            pltpu.VMEM((4 * samples, depth), jnp.bfloat16),
            pltpu.VMEM((tiles, depth, width), jnp.bfloat16),
            pltpu.VMEM((beams, half), jnp.bfloat16),
            pltpu.VMEM((2, stations, LANES), f32),
            pltpu.VMEM((32, entries), f32),
            pltpu.VMEM((tiles, 8, width), f32),
            pltpu.VMEM((n // 2, 8, LANES), f32),
            pltpu.VMEM((n // 2, 8, LANES), f32),
            pltpu.SemaphoreType.DMA((7,)),
            pltpu.SemaphoreType.DMA((n,)),
            pltpu.SemaphoreType.DMA((n,)),
            pltpu.SemaphoreType.DMA((blocks,)),
            pltpu.SemaphoreType.DMA((blocks,)),
            pltpu.SemaphoreType.DMA((n,)),
            pltpu.SemaphoreType.DMA((n,)),
            pltpu.SemaphoreType.DMA,
        ],
        compiler_params=pltpu.CompilerParams(
            collective_id=0, has_side_effects=True, vmem_limit_bytes=40 * 2**20
        ),
    )(
        *(
            pltpu.with_memory_space_constraint(operand, pltpu.HBM)
            for operand in (
                voltages,
                cal_num,
                cal_weight,
                flags,
                positions,
                directions,
                pointing.reshape(tiles, 1, width),
            )
        )
    )
    return jnp.transpose(power, (1, 0, 2)), gains


def solution(mesh):
    return jax.shard_map(
        body,
        mesh=mesh,
        in_specs=(
            P(("group", "chan"), None, None, None),
            P(("group", "chan"), None, None),
            P(("group", "chan"), None, None),
            P(("group", "chan"), None),
            P(),
            P(),
            P("group"),
        ),
        out_specs=(P(("group", "chan"), None, None), P(("group", "chan"), None, None)),
        check_vma=False,
    )
```

```python
import functools
import jax
import jax.numpy as jnp
from jax import lax
from jax.experimental import pallas as pl
from jax.experimental.pallas import tpu as pltpu
from jax.sharding import PartitionSpec as P

ITERS = 8
PENALTY = 2.0
RIDGE = 1.0
ORDER = 4
LANES = 128
ROUNDING = 1.5 * 2.0**23
SINE = (4.44287957, -7.30781668, 3.59777418, -0.79119939)
COSINE = (1.4142135, -6.97885095, 5.73946038, -1.88355791, 0.31068803)


def basis_at(place):
    return (
        1.0,
        place,
        0.5 * (3.0 * place * place - 1.0),
        0.5 * (5.0 * place * place * place - 3.0 * place),
    )


def invert_small(matrix):
    order = len(matrix)
    unit = jnp.ones_like(matrix[0][0])
    nothing = jnp.zeros_like(unit)
    left = [list(line) for line in matrix]
    right = [[unit if row == col else nothing for col in range(order)] for row in range(order)]
    for pivot in range(order):
        factor = 1.0 / left[pivot][pivot]
        left[pivot] = [entry * factor for entry in left[pivot]]
        right[pivot] = [entry * factor for entry in right[pivot]]
        for row in range(order):
            if row != pivot:
                scale = left[row][pivot]
                left[row] = [a - scale * b for a, b in zip(left[row], left[pivot])]
                right[row] = [a - scale * b for a, b in zip(right[row], right[pivot])]
    return right


def horner(coefficients, value):
    total = coefficients[-1] * value + coefficients[-2]
    for entry in coefficients[-3::-1]:
        total = total * value + entry
    return total


def tile_at(step, mine, tiles):
    if tiles == 4:
        high = lax.rem(mine // 2 + 1 - step // 2, 2)
        low = lax.rem(lax.rem(mine, 2) + (step + 1) // 2, 2)
        return 2 * high + low
    return lax.rem(mine + tiles // 2 + step, tiles)


def combine(factors, terms):
    total = terms[0] * factors[0]
    for factor, term in zip(factors[1:], terms[1:]):
        total = total + factor * term
    return total


def tree(terms):
    while len(terms) > 1:
        terms = [sum(terms[at : at + 2]) if at + 1 < len(terms) else terms[at] for at in range(0, len(terms), 2)]
    return terms[0]


def kernel(
    n,
    tiles,
    volts_hbm,
    num_hbm,
    weight_hbm,
    flags_hbm,
    positions_hbm,
    directions_hbm,
    pointing_hbm,
    power_ref,
    gains_ref,
    num_ref,
    weight_ref,
    flags_ref,
    positions_ref,
    directions_ref,
    pointing_ref,
    volts,
    message,
    gathered,
    outbox,
    inbox,
    ordered,
    products,
    phasors,
    ready,
    columns,
    table,
    pointed,
    local_ref,
    dual_ref,
    load_sem,
    cal_send,
    cal_recv,
    fit_send,
    fit_recv,
    out_send,
    out_recv,
    own_sem,
):
    me = lax.axis_index("chan")
    stations = flags_ref.shape[1]
    blocks = stations // LANES
    width = phasors.shape[2]
    samples = volts.shape[1]
    half = samples // 2
    per_device = ready.shape[0] // n
    per_tile = n // tiles
    share = lax.rem(me, blocks)

    loads = [
        pltpu.make_async_copy(source, target, load_sem.at[index])
        for index, (source, target) in enumerate(
            (
                (num_hbm.at[0], num_ref),
                (weight_hbm.at[0], weight_ref),
                (flags_hbm, flags_ref),
                (positions_hbm, positions_ref),
                (directions_hbm, directions_ref),
                (pointing_hbm, pointing_ref),
                (volts_hbm.at[0], volts),
            )
        )
    ]
    for load in loads:
        load.start()

    barrier = pltpu.get_barrier_semaphore()

    def far_first(offset):
        return 1 + lax.rem(offset + n // 2 - 2, n - 1)

    @pl.loop(1, n)
    def _(offset):
        pl.semaphore_signal(
            barrier,
            inc=1,
            device_id={"chan": lax.rem(me + far_first(offset), n)},
            device_id_type=pl.DeviceIdType.MESH,
        )

    for load in loads[:3]:
        load.wait()
    for block in range(blocks):
        lanes = pl.ds(block * LANES, LANES)
        mask = flags_ref[:, lanes].astype(jnp.float32)
        message[block, 0:4, :] = mask * num_ref[:, lanes]
        for row in range(4):
            message[block, pl.ds(4 + row, 1), :] = mask * weight_ref[pl.ds(row // 2, 1), lanes]
    gathered[me] = message[share]

    pl.semaphore_wait(barrier, n - 1)

    def cal_copy(block, slot, peer, sent, received):
        return pltpu.make_async_remote_copy(
            src_ref=message.at[block],
            dst_ref=gathered.at[slot],
            send_sem=cal_send.at[sent],
            recv_sem=cal_recv.at[received],
            device_id={"chan": peer},
            device_id_type=pl.DeviceIdType.MESH,
        )

    @pl.loop(1, n)
    def _(offset):
        peer = lax.rem(me + far_first(offset), n)
        cal_copy(lax.rem(peer, blocks), me, peer, peer, me).start()

    for load in loads[3:6]:
        load.wait()
    for axis in range(2):
        for block in range(blocks):
            lanes = pl.ds(block * LANES, LANES)
            row = jnp.broadcast_to(positions_ref[pl.ds(axis, 1), lanes], (LANES, LANES))
            columns[axis, lanes, :] = row.T

    rest = directions_ref[...]
    table[...] = jnp.zeros_like(table)
    for term in range(3):
        head = rest.astype(jnp.bfloat16).astype(jnp.float32)
        table[pl.ds(8 * term, 2), :] = head
        rest = rest - head
    ratio = 1.0 + 0.15 * (2.0 * (me.astype(jnp.float32) + 0.5) / n)
    entries = directions_ref.shape[1]
    chunk = 32

    @pl.loop(0, tiles)
    def _(tile):
        numbers = lax.broadcasted_iota(jnp.int32, (entries, width), 0)
        chosen = jnp.where(numbers == pointing_ref[tile], 1.0, 0.0).astype(jnp.bfloat16)
        terms = table[...].astype(jnp.bfloat16)
        found = jnp.dot(terms, chosen, preferred_element_type=jnp.float32)
        pointed[tile] = (found[0:8] + found[8:16] + found[16:24]) * ratio

    def make_phasors(step):
        tile = tile_at(step, me // per_tile, tiles)
        east = pointed[tile, 0:1, :]
        north = pointed[tile, 1:2, :]

        @pl.loop(0, stations // chunk)
        def _(part):
            rows = pl.ds(pl.multiple_of(part * chunk, chunk), chunk)
            below = pl.ds(pl.multiple_of(stations + part * chunk, chunk), chunk)
            for piece in range(width // LANES):
                lanes = pl.ds(piece * LANES, LANES)
                cut = slice(piece * LANES, (piece + 1) * LANES)
                turns = columns[0, rows, :] * east[:, cut] + columns[1, rows, :] * north[:, cut]
                turns = turns - ((turns + ROUNDING) - ROUNDING)
                square = turns * turns
                sine = horner(SINE, square) * turns
                cosine = horner(COSINE, square)
                phasors[step, rows, lanes] = (1.0 - sine * sine).astype(jnp.bfloat16)
                phasors[step, below, lanes] = (sine * cosine).astype(jnp.bfloat16)

    make_phasors(0)

    @pl.loop(1, n)
    def _(offset):
        peer = lax.rem(me + offset, n)
        cal_copy(0, peer, peer, peer, peer).wait_recv()

    pairs = n // 2
    basis = [basis_at(2.0 * (n - pair - 0.5) / n - 1.0) for pair in range(pairs)]
    sign = jnp.where(lax.broadcasted_iota(jnp.int32, (8, LANES), 0) < 4, 1.0, -1.0)
    solve_rows = []
    for pair in range(pairs):
        first = gathered[n - 1 - pair]
        second = gathered[pair]
        weight = jnp.concatenate([first[4:8], second[4:8]], axis=0)
        usable = jnp.where(weight > 0.0, 1.0, 0.0)
        damping = 1.0 / (weight + PENALTY)
        target = jnp.concatenate([first[0:4], second[0:4]], axis=0) * damping
        solve_rows.append((usable, PENALTY * damping, target))

    def both(term, value):
        value = value * sign if term % 2 else value
        return value + pltpu.roll(value, 4, 0)

    gram = [[None] * ORDER for _ in range(ORDER)]
    for first in range(ORDER):
        for second in range(first, ORDER):
            terms = [
                (basis[pair][first] * basis[pair][second]) * solve_rows[pair][0]
                for pair in range(pairs)
            ]
            gram[first][second] = both(first + second, tree(terms))
            gram[second][first] = gram[first][second]
        gram[first][first] = gram[first][first] + RIDGE
    inverse = invert_small(gram)
    local_ref[...] = jnp.zeros_like(local_ref)
    dual_ref[...] = jnp.zeros_like(dual_ref)
    nothing = jnp.zeros((8, LANES), jnp.float32)

    def sweep(_, line):
        signed = [entry * sign if term % 2 else entry for term, entry in enumerate(line)]
        numerator = [[] for _ in range(ORDER)]
        for pair in range(pairs):
            values = basis[pair]
            usable, damping, target = solve_rows[pair]
            fitted = tree([signed[0]] + [values[term] * signed[term] for term in range(1, ORDER)])
            dual = dual_ref[pair] + usable * (local_ref[pair] - fitted)
            local = target + damping * (fitted - dual)
            local_ref[pair] = local
            dual_ref[pair] = dual
            summand = usable * (local + dual)
            for term in range(ORDER):
                numerator[term].append(values[term] * summand if term else summand)
        sums = [both(term, tree(terms)) for term, terms in enumerate(numerator)]
        return tuple(
            tree([entry * total for entry, total in zip(inverse[first], sums)])
            for first in range(ORDER)
        )

    line = lax.fori_loop(0, ITERS, sweep, (nothing,) * ORDER)
    line = [entry[0:4] for entry in line]

    def fitted_at(channel):
        return combine(basis_at(2.0 * (channel.astype(jnp.float32) + 0.5) / n - 1.0), line)

    def fit_copy(source, slot, peer, sent, received):
        return pltpu.make_async_remote_copy(
            src_ref=outbox.at[source],
            dst_ref=inbox.at[slot],
            send_sem=fit_send.at[sent],
            recv_sem=fit_recv.at[received],
            device_id={"chan": peer},
            device_id_type=pl.DeviceIdType.MESH,
        )

    for offset in range(1, blocks):
        mate = lax.rem(share + offset, blocks)
        peer = me - share + mate
        outbox[mate] = fitted_at(peer)
        fit_copy(mate, share, peer, mate, share).start()
    inbox[share] = fitted_at(me)

    loads[6].wait()
    row = lax.broadcasted_iota(jnp.int32, (samples, samples), 0)
    col = lax.broadcasted_iota(jnp.int32, (samples, samples), 1)
    origin = jnp.where(row < half, 2 * row, 2 * (row - half) + 1)
    shuffle = jnp.where(col == origin, 1.0, 0.0).astype(jnp.bfloat16)
    for polar in range(2):
        ordered[polar] = jnp.dot(shuffle, volts[polar], preferred_element_type=jnp.float32)

    make_phasors(1)
    for offset in range(1, blocks):
        mate = lax.rem(share + offset, blocks)
        fit_copy(mate, mate, me - share + mate, mate, mate).wait_recv()
    for block in range(blocks):
        gains_ref[0, :, pl.ds(block * LANES, LANES)] = inbox[block]

    scale = flags_ref[...].astype(jnp.float32) * stations ** (-0.5)
    strip = 64
    for polar in range(2):
        gain_re = gains_ref[0, pl.ds(2 * polar, 1), :] * scale
        gain_im = gains_ref[0, pl.ds(2 * polar + 1, 1), :] * scale

        @pl.loop(0, samples // strip)
        def _(step):
            rows = pl.ds(pl.multiple_of(step * strip, strip), strip)
            real = ordered[polar, rows, :stations]
            imag = ordered[polar, rows, stations:]
            new_re = (gain_re * real + gain_im * imag).astype(jnp.bfloat16)
            new_im = (gain_re * imag - gain_im * real).astype(jnp.bfloat16)
            upper = pl.ds(pl.multiple_of(2 * polar * samples + step * strip, strip), strip)
            lower = pl.ds(pl.multiple_of((2 * polar + 1) * samples + step * strip, strip), strip)
            products[upper, :stations] = new_re
            products[upper, stations:] = new_im
            products[lower, :stations] = new_im
            products[lower, stations:] = -new_re

    def out_copy(owner, source, sent, received):
        rows = pl.ds(pl.multiple_of(owner * per_device, per_device), per_device)
        return pltpu.make_async_remote_copy(
            src_ref=ready.at[rows, :],
            dst_ref=power_ref.at[source],
            send_sem=out_send.at[sent],
            recv_sem=out_recv.at[received],
            device_id={"chan": owner},
            device_id_type=pl.DeviceIdType.MESH,
        )

    def own_copy():
        rows = pl.ds(pl.multiple_of(me * per_device, per_device), per_device)
        return pltpu.make_async_copy(ready.at[rows, :], power_ref.at[me], own_sem)

    @pl.loop(0, tiles)
    def _(step):
        @pl.when(step >= 2)
        def _():
            make_phasors(step)

        tile = tile_at(step, me // per_tile, tiles)
        beams = jnp.dot(products[...], phasors[step], preferred_element_type=jnp.float32)
        total = beams[:samples] * beams[:samples]
        for part in range(1, 4):
            piece = beams[part * samples : (part + 1) * samples]
            total = total + piece * piece
        mean = (total[:half] + total[half:]) * 0.5
        rows = pl.ds(pl.multiple_of(tile * width, width), width)
        ready[rows, :] = mean.T.astype(jnp.bfloat16)

        @pl.loop(0, per_tile)
        def _(index):
            owner = tile * per_tile + index

            @pl.when(owner != me)
            def _():
                out_copy(owner, me, owner, me).start()

            @pl.when(owner == me)
            def _():
                own_copy().start()

    own_copy().wait()
    for offset in range(1, blocks):
        mate = lax.rem(share + offset, blocks)
        fit_copy(mate, share, me - share + mate, mate, share).wait_send()

    @pl.loop(1, n)
    def _(offset):
        peer = lax.rem(me + offset, n)
        cal_copy(lax.rem(peer, blocks), me, peer, peer, me).wait_send()
        out_copy(peer, me, peer, me).wait_send()

    @pl.loop(1, n)
    def _(offset):
        peer = lax.rem(me + offset, n)
        out_copy(peer, peer, peer, peer).wait_recv()


def body(voltages, cal_num, cal_weight, flags, positions, directions, pointing):
    n = lax.axis_size("chan")
    count, polars, samples, depth = voltages.shape
    stations = flags.shape[1]
    blocks = stations // LANES
    assert count == 1 and polars == 2 and n % blocks == 0 and n % 2 == 0
    beams = pointing.shape[0]
    tiles = 4
    width = beams // tiles
    half = samples // 2
    entries = directions.shape[1]
    vmem = pl.BlockSpec(memory_space=pltpu.VMEM)
    hbm = pl.BlockSpec(memory_space=pltpu.HBM)
    f32 = jnp.float32
    power, gains = pl.pallas_call(
        functools.partial(kernel, n, tiles),
        out_shape=(
            pltpu.VMEM((n, beams // n, half), jnp.bfloat16),
            jax.ShapeDtypeStruct(cal_num.shape, f32),
        ),
        in_specs=[hbm] * 7,
        out_specs=(vmem, vmem),
        scratch_shapes=[
            pltpu.VMEM(cal_num.shape[1:], f32),
            pltpu.VMEM(cal_weight.shape[1:], f32),
            pltpu.VMEM(flags.shape, jnp.int32),
            pltpu.VMEM(positions.shape, f32),
            pltpu.VMEM(directions.shape, f32),
            pltpu.VMEM((tiles, 1, width), jnp.int32),
            pltpu.VMEM((polars, samples, depth), jnp.bfloat16),
            pltpu.VMEM((blocks, 8, LANES), f32),
            pltpu.VMEM((n, 8, LANES), f32),
            pltpu.VMEM((blocks, 4, LANES), f32),
            pltpu.VMEM((blocks, 4, LANES), f32),
            pltpu.VMEM((polars, samples, depth), f32),
            pltpu.VMEM((4 * samples, depth), jnp.bfloat16),
            pltpu.VMEM((tiles, depth, width), jnp.bfloat16),
            pltpu.VMEM((beams, half), jnp.bfloat16),
            pltpu.VMEM((2, stations, LANES), f32),
            pltpu.VMEM((32, entries), f32),
            pltpu.VMEM((tiles, 8, width), f32),
            pltpu.VMEM((n // 2, 8, LANES), f32),
            pltpu.VMEM((n // 2, 8, LANES), f32),
            pltpu.SemaphoreType.DMA((7,)),
            pltpu.SemaphoreType.DMA((n,)),
            pltpu.SemaphoreType.DMA((n,)),
            pltpu.SemaphoreType.DMA((blocks,)),
            pltpu.SemaphoreType.DMA((blocks,)),
            pltpu.SemaphoreType.DMA((n,)),
            pltpu.SemaphoreType.DMA((n,)),
            pltpu.SemaphoreType.DMA,
        ],
        compiler_params=pltpu.CompilerParams(
            collective_id=0, has_side_effects=True, vmem_limit_bytes=40 * 2**20
        ),
    )(
        *(
            pltpu.with_memory_space_constraint(operand, pltpu.HBM)
            for operand in (
                voltages,
                cal_num,
                cal_weight,
                flags,
                positions,
                directions,
                pointing.reshape(tiles, 1, width),
            )
        )
    )
    return jnp.transpose(power, (1, 0, 2)), gains


def solution(mesh):
    return jax.shard_map(
        body,
        mesh=mesh,
        in_specs=(
            P(("group", "chan"), None, None, None),
            P(("group", "chan"), None, None),
            P(("group", "chan"), None, None),
            P(("group", "chan"), None),
            P(),
            P(),
            P("group"),
        ),
        out_specs=(P(("group", "chan"), None, None), P(("group", "chan"), None, None)),
        check_vma=False,
    )
```

```python
import functools
import jax
import jax.numpy as jnp
from jax import lax
from jax.experimental import pallas as pl
from jax.experimental.pallas import tpu as pltpu
from jax.sharding import PartitionSpec as P

ITERS = 8
PENALTY = 2.0
RIDGE = 1.0
ORDER = 4
LANES = 128
ROUNDING = 1.5 * 2.0**23
SINE = (4.44288292, -7.30824569, 3.60635422, -0.84611165, 0.10982452)
COSINE = (1.4142135, -6.97885095, 5.73946038, -1.88355791, 0.31068803)


def basis_at(place):
    return (
        1.0,
        place,
        0.5 * (3.0 * place * place - 1.0),
        0.5 * (5.0 * place * place * place - 3.0 * place),
    )


def invert_small(matrix):
    order = len(matrix)
    unit = jnp.ones_like(matrix[0][0])
    nothing = jnp.zeros_like(unit)
    left = [list(line) for line in matrix]
    right = [[unit if row == col else nothing for col in range(order)] for row in range(order)]
    for pivot in range(order):
        factor = 1.0 / left[pivot][pivot]
        left[pivot] = [entry * factor for entry in left[pivot]]
        right[pivot] = [entry * factor for entry in right[pivot]]
        for row in range(order):
            if row != pivot:
                scale = left[row][pivot]
                left[row] = [a - scale * b for a, b in zip(left[row], left[pivot])]
                right[row] = [a - scale * b for a, b in zip(right[row], right[pivot])]
    return right


def horner(coefficients, value):
    total = coefficients[-1] * value + coefficients[-2]
    for entry in coefficients[-3::-1]:
        total = total * value + entry
    return total


def tile_at(step, mine, tiles):
    if tiles == 4:
        high = lax.rem(mine // 2 + 1 - step // 2, 2)
        low = lax.rem(lax.rem(mine, 2) + (step + 1) // 2, 2)
        return 2 * high + low
    return lax.rem(mine + tiles // 2 + step, tiles)


def combine(factors, terms):
    total = terms[0] * factors[0]
    for factor, term in zip(factors[1:], terms[1:]):
        total = total + factor * term
    return total


def tree(terms):
    while len(terms) > 1:
        terms = [sum(terms[at : at + 2]) if at + 1 < len(terms) else terms[at] for at in range(0, len(terms), 2)]
    return terms[0]


def kernel(
    n,
    tiles,
    volts_hbm,
    num_hbm,
    weight_hbm,
    flags_hbm,
    positions_hbm,
    directions_hbm,
    pointing_hbm,
    power_ref,
    gains_ref,
    num_ref,
    weight_ref,
    flags_ref,
    positions_ref,
    directions_ref,
    pointing_ref,
    volts,
    message,
    gathered,
    outbox,
    inbox,
    ordered,
    products,
    phasors,
    ready,
    columns,
    table,
    pointed,
    local_ref,
    dual_ref,
    load_sem,
    cal_send,
    cal_recv,
    fit_send,
    fit_recv,
    out_send,
    out_recv,
    own_sem,
):
    me = lax.axis_index("chan")
    stations = flags_ref.shape[1]
    blocks = stations // LANES
    width = phasors.shape[2] // 2
    samples = volts.shape[1]
    half = samples // 2
    per_device = ready.shape[0] // n
    per_tile = n // tiles
    share = lax.rem(me, blocks)

    loads = [
        pltpu.make_async_copy(source, target, load_sem.at[index])
        for index, (source, target) in enumerate(
            (
                (num_hbm.at[0], num_ref),
                (weight_hbm.at[0], weight_ref),
                (flags_hbm, flags_ref),
                (positions_hbm, positions_ref),
                (directions_hbm, directions_ref),
                (pointing_hbm, pointing_ref),
                (volts_hbm.at[0], volts),
            )
        )
    ]
    for load in loads:
        load.start()

    barrier = pltpu.get_barrier_semaphore()

    @pl.loop(1, n)
    def _(offset):
        pl.semaphore_signal(
            barrier,
            inc=1,
            device_id={"chan": lax.rem(me + offset, n)},
            device_id_type=pl.DeviceIdType.MESH,
        )

    for load in loads[:3]:
        load.wait()
    for block in range(blocks):
        lanes = pl.ds(block * LANES, LANES)
        mask = flags_ref[:, lanes].astype(jnp.float32)
        message[block, 0:4, :] = mask * num_ref[:, lanes]
        for row in range(4):
            message[block, pl.ds(4 + row, 1), :] = mask * weight_ref[pl.ds(row // 2, 1), lanes]
    gathered[me] = message[share]

    pl.semaphore_wait(barrier, n - 1)

    def cal_copy(block, slot, peer, sent, received):
        return pltpu.make_async_remote_copy(
            src_ref=message.at[block],
            dst_ref=gathered.at[slot],
            send_sem=cal_send.at[sent],
            recv_sem=cal_recv.at[received],
            device_id={"chan": peer},
            device_id_type=pl.DeviceIdType.MESH,
        )

    @pl.loop(1, n)
    def _(offset):
        peer = lax.rem(me + offset, n)
        cal_copy(lax.rem(peer, blocks), me, peer, peer, me).start()

    for load in loads[3:6]:
        load.wait()
    for axis in range(2):
        for block in range(blocks):
            lanes = pl.ds(block * LANES, LANES)
            row = jnp.broadcast_to(positions_ref[pl.ds(axis, 1), lanes], (LANES, LANES))
            columns[axis, lanes, :] = row.T

    rest = directions_ref[...]
    table[...] = jnp.zeros_like(table)
    for term in range(3):
        head = rest.astype(jnp.bfloat16).astype(jnp.float32)
        table[pl.ds(8 * term, 2), :] = head
        rest = rest - head
    ratio = 1.0 + 0.15 * (2.0 * (me.astype(jnp.float32) + 0.5) / n)
    entries = directions_ref.shape[1]
    chunk = 32

    @pl.loop(0, tiles)
    def _(tile):
        numbers = lax.broadcasted_iota(jnp.int32, (entries, width), 0)
        chosen = jnp.where(numbers == pointing_ref[tile], 1.0, 0.0).astype(jnp.bfloat16)
        terms = table[...].astype(jnp.bfloat16)
        found = jnp.dot(terms, chosen, preferred_element_type=jnp.float32)
        pointed[tile] = (found[0:8] + found[8:16] + found[16:24]) * ratio

    def make_phasors(step):
        group, side = step // 2, step % 2
        tile = tile_at(step, me // per_tile, tiles)
        east = pointed[tile, 0:1, :]
        north = pointed[tile, 1:2, :]

        @pl.loop(0, stations // chunk)
        def _(part):
            rows = pl.ds(pl.multiple_of(part * chunk, chunk), chunk)
            below = pl.ds(pl.multiple_of(stations + part * chunk, chunk), chunk)
            for piece in range(width // LANES):
                lanes = pl.ds(side * width + piece * LANES, LANES)
                cut = slice(piece * LANES, (piece + 1) * LANES)
                turns = columns[0, rows, :] * east[:, cut] + columns[1, rows, :] * north[:, cut]
                turns = turns - ((turns + ROUNDING) - ROUNDING)
                square = turns * turns
                sine = horner(SINE, square) * turns
                cosine = horner(COSINE, square)
                phasors[group, rows, lanes] = (1.0 - sine * sine).astype(jnp.bfloat16)
                phasors[group, below, lanes] = (sine * cosine).astype(jnp.bfloat16)

    make_phasors(0)

    @pl.loop(1, n)
    def _(offset):
        peer = lax.rem(me + offset, n)
        cal_copy(0, peer, peer, peer, peer).wait_recv()

    pairs = n // 2
    basis = [basis_at(2.0 * (n - pair - 0.5) / n - 1.0) for pair in range(pairs)]
    sign = jnp.where(lax.broadcasted_iota(jnp.int32, (8, LANES), 0) < 4, 1.0, -1.0)
    solve_rows = []
    for pair in range(pairs):
        first = gathered[n - 1 - pair]
        second = gathered[pair]
        weight = jnp.concatenate([first[4:8], second[4:8]], axis=0)
        usable = jnp.where(weight > 0.0, 1.0, 0.0)
        damping = 1.0 / (weight + PENALTY)
        target = jnp.concatenate([first[0:4], second[0:4]], axis=0) * damping
        solve_rows.append((usable, PENALTY * damping, target))

    def both(term, value):
        value = value * sign if term % 2 else value
        return value + pltpu.roll(value, 4, 0)

    gram = [[None] * ORDER for _ in range(ORDER)]
    for first in range(ORDER):
        for second in range(first, ORDER):
            terms = [
                (basis[pair][first] * basis[pair][second]) * solve_rows[pair][0]
                for pair in range(pairs)
            ]
            gram[first][second] = both(first + second, tree(terms))
            gram[second][first] = gram[first][second]
        gram[first][first] = gram[first][first] + RIDGE
    inverse = invert_small(gram)
    local_ref[...] = jnp.zeros_like(local_ref)
    dual_ref[...] = jnp.zeros_like(dual_ref)
    nothing = jnp.zeros((8, LANES), jnp.float32)

    def sweep(_, line):
        signed = [entry * sign if term % 2 else entry for term, entry in enumerate(line)]
        numerator = [[] for _ in range(ORDER)]
        for pair in range(pairs):
            values = basis[pair]
            usable, damping, target = solve_rows[pair]
            fitted = tree([signed[0]] + [values[term] * signed[term] for term in range(1, ORDER)])
            dual = dual_ref[pair] + usable * (local_ref[pair] - fitted)
            local = target + damping * (fitted - dual)
            local_ref[pair] = local
            dual_ref[pair] = dual
            summand = usable * (local + dual)
            for term in range(ORDER):
                numerator[term].append(values[term] * summand if term else summand)
        sums = [both(term, tree(terms)) for term, terms in enumerate(numerator)]
        return tuple(
            tree([entry * total for entry, total in zip(inverse[first], sums)])
            for first in range(ORDER)
        )

    line = lax.fori_loop(0, ITERS, sweep, (nothing,) * ORDER)
    line = [entry[0:4] for entry in line]

    def fitted_at(channel):
        return combine(basis_at(2.0 * (channel.astype(jnp.float32) + 0.5) / n - 1.0), line)

    def fit_copy(source, slot, peer, sent, received):
        return pltpu.make_async_remote_copy(
            src_ref=outbox.at[source],
            dst_ref=inbox.at[slot],
            send_sem=fit_send.at[sent],
            recv_sem=fit_recv.at[received],
            device_id={"chan": peer},
            device_id_type=pl.DeviceIdType.MESH,
        )

    for offset in range(1, blocks):
        mate = lax.rem(share + offset, blocks)
        peer = me - share + mate
        outbox[mate] = fitted_at(peer)
        fit_copy(mate, share, peer, mate, share).start()
    inbox[share] = fitted_at(me)

    loads[6].wait()
    row = lax.broadcasted_iota(jnp.int32, (samples, samples), 0)
    col = lax.broadcasted_iota(jnp.int32, (samples, samples), 1)
    origin = jnp.where(row < half, 2 * row, 2 * (row - half) + 1)
    shuffle = jnp.where(col == origin, 1.0, 0.0).astype(jnp.bfloat16)
    for polar in range(2):
        ordered[polar] = jnp.dot(shuffle, volts[polar], preferred_element_type=jnp.float32)

    make_phasors(1)
    for offset in range(1, blocks):
        mate = lax.rem(share + offset, blocks)
        fit_copy(mate, mate, me - share + mate, mate, mate).wait_recv()
    for block in range(blocks):
        gains_ref[0, :, pl.ds(block * LANES, LANES)] = inbox[block]

    scale = flags_ref[...].astype(jnp.float32) * stations ** (-0.5)
    strip = 64
    for polar in range(2):
        gain_re = gains_ref[0, pl.ds(2 * polar, 1), :] * scale
        gain_im = gains_ref[0, pl.ds(2 * polar + 1, 1), :] * scale

        @pl.loop(0, samples // strip)
        def _(step):
            rows = pl.ds(pl.multiple_of(step * strip, strip), strip)
            real = ordered[polar, rows, :stations]
            imag = ordered[polar, rows, stations:]
            new_re = (gain_re * real + gain_im * imag).astype(jnp.bfloat16)
            new_im = (gain_re * imag - gain_im * real).astype(jnp.bfloat16)
            upper = pl.ds(pl.multiple_of(2 * polar * samples + step * strip, strip), strip)
            lower = pl.ds(pl.multiple_of((2 * polar + 1) * samples + step * strip, strip), strip)
            products[upper, :stations] = new_re
            products[upper, stations:] = new_im
            products[lower, :stations] = new_im
            products[lower, stations:] = -new_re

    def out_copy(owner, source, sent, received):
        rows = pl.ds(pl.multiple_of(owner * per_device, per_device), per_device)
        return pltpu.make_async_remote_copy(
            src_ref=ready.at[rows, :],
            dst_ref=power_ref.at[source],
            send_sem=out_send.at[sent],
            recv_sem=out_recv.at[received],
            device_id={"chan": owner},
            device_id_type=pl.DeviceIdType.MESH,
        )

    def own_copy():
        rows = pl.ds(pl.multiple_of(me * per_device, per_device), per_device)
        return pltpu.make_async_copy(ready.at[rows, :], power_ref.at[me], own_sem)

    @pl.loop(0, tiles // 2)
    def _(group):
        @pl.when(group > 0)
        def _():
            for step in range(2, tiles):
                make_phasors(step)

        beams = jnp.dot(products[...], phasors[group], preferred_element_type=jnp.float32)
        total = beams[:samples] * beams[:samples]
        for part in range(1, 4):
            piece = beams[part * samples : (part + 1) * samples]
            total = total + piece * piece
        mean = (total[:half] + total[half:]) * 0.5
        for side in range(2):
            tile = tile_at(2 * group + side, me // per_tile, tiles)
            rows = pl.ds(pl.multiple_of(tile * width, width), width)
            own = mean[:, side * width : (side + 1) * width]
            ready[rows, :] = own.T.astype(jnp.bfloat16)

            @pl.loop(0, per_tile)
            def _(index):
                owner = tile * per_tile + index

                @pl.when(owner != me)
                def _():
                    out_copy(owner, me, owner, me).start()

                @pl.when(owner == me)
                def _():
                    own_copy().start()

    own_copy().wait()
    for offset in range(1, blocks):
        mate = lax.rem(share + offset, blocks)
        fit_copy(mate, share, me - share + mate, mate, share).wait_send()

    @pl.loop(1, n)
    def _(offset):
        peer = lax.rem(me + offset, n)
        cal_copy(lax.rem(peer, blocks), me, peer, peer, me).wait_send()
        out_copy(peer, me, peer, me).wait_send()
        out_copy(peer, peer, peer, peer).wait_recv()


def body(voltages, cal_num, cal_weight, flags, positions, directions, pointing):
    n = lax.axis_size("chan")
    count, polars, samples, depth = voltages.shape
    stations = flags.shape[1]
    blocks = stations // LANES
    assert count == 1 and polars == 2 and n % blocks == 0 and n % 2 == 0
    beams = pointing.shape[0]
    tiles = 4
    width = beams // tiles
    half = samples // 2
    entries = directions.shape[1]
    vmem = pl.BlockSpec(memory_space=pltpu.VMEM)
    hbm = pl.BlockSpec(memory_space=pltpu.HBM)
    f32 = jnp.float32
    power, gains = pl.pallas_call(
        functools.partial(kernel, n, tiles),
        out_shape=(
            pltpu.VMEM((n, beams // n, half), jnp.bfloat16),
            jax.ShapeDtypeStruct(cal_num.shape, f32),
        ),
        in_specs=[hbm] * 7,
        out_specs=(vmem, vmem),
        scratch_shapes=[
            pltpu.VMEM(cal_num.shape[1:], f32),
            pltpu.VMEM(cal_weight.shape[1:], f32),
            pltpu.VMEM(flags.shape, jnp.int32),
            pltpu.VMEM(positions.shape, f32),
            pltpu.VMEM(directions.shape, f32),
            pltpu.VMEM((tiles, 1, width), jnp.int32),
            pltpu.VMEM((polars, samples, depth), jnp.bfloat16),
            pltpu.VMEM((blocks, 8, LANES), f32),
            pltpu.VMEM((n, 8, LANES), f32),
            pltpu.VMEM((blocks, 4, LANES), f32),
            pltpu.VMEM((blocks, 4, LANES), f32),
            pltpu.VMEM((polars, samples, depth), f32),
            pltpu.VMEM((4 * samples, depth), jnp.bfloat16),
            pltpu.VMEM((tiles // 2, depth, 2 * width), jnp.bfloat16),
            pltpu.VMEM((beams, half), jnp.bfloat16),
            pltpu.VMEM((2, stations, LANES), f32),
            pltpu.VMEM((32, entries), f32),
            pltpu.VMEM((tiles, 8, width), f32),
            pltpu.VMEM((n // 2, 8, LANES), f32),
            pltpu.VMEM((n // 2, 8, LANES), f32),
            pltpu.SemaphoreType.DMA((7,)),
            pltpu.SemaphoreType.DMA((n,)),
            pltpu.SemaphoreType.DMA((n,)),
            pltpu.SemaphoreType.DMA((blocks,)),
            pltpu.SemaphoreType.DMA((blocks,)),
            pltpu.SemaphoreType.DMA((n,)),
            pltpu.SemaphoreType.DMA((n,)),
            pltpu.SemaphoreType.DMA,
        ],
        compiler_params=pltpu.CompilerParams(
            collective_id=0, has_side_effects=True, vmem_limit_bytes=40 * 2**20
        ),
    )(
        *(
            pltpu.with_memory_space_constraint(operand, pltpu.HBM)
            for operand in (
                voltages,
                cal_num,
                cal_weight,
                flags,
                positions,
                directions,
                pointing.reshape(tiles, 1, width),
            )
        )
    )
    return jnp.transpose(power, (1, 0, 2)), gains


def solution(mesh):
    return jax.shard_map(
        body,
        mesh=mesh,
        in_specs=(
            P(("group", "chan"), None, None, None),
            P(("group", "chan"), None, None),
            P(("group", "chan"), None, None),
            P(("group", "chan"), None),
            P(),
            P(),
            P("group"),
        ),
        out_specs=(P(("group", "chan"), None, None), P(("group", "chan"), None, None)),
        check_vma=False,
    )
```

```python
import functools
import jax
import jax.numpy as jnp
from jax import lax
from jax.experimental import pallas as pl
from jax.experimental.pallas import tpu as pltpu
from jax.sharding import PartitionSpec as P

ITERS = 8
PENALTY = 2.0
RIDGE = 1.0
ORDER = 4
LANES = 128
ROUNDING = 1.5 * 2.0**23
SINE = (4.44288292, -7.30824569, 3.60635422, -0.84611165, 0.10982452)
COSINE = (1.4142135, -6.97885095, 5.73946038, -1.88355791, 0.31068803)


def basis_at(place):
    return (
        1.0,
        place,
        0.5 * (3.0 * place * place - 1.0),
        0.5 * (5.0 * place * place * place - 3.0 * place),
    )


def invert_small(matrix):
    order = len(matrix)
    unit = jnp.ones_like(matrix[0][0])
    nothing = jnp.zeros_like(unit)
    left = [list(line) for line in matrix]
    right = [[unit if row == col else nothing for col in range(order)] for row in range(order)]
    for pivot in range(order):
        factor = 1.0 / left[pivot][pivot]
        left[pivot] = [entry * factor for entry in left[pivot]]
        right[pivot] = [entry * factor for entry in right[pivot]]
        for row in range(order):
            if row != pivot:
                scale = left[row][pivot]
                left[row] = [a - scale * b for a, b in zip(left[row], left[pivot])]
                right[row] = [a - scale * b for a, b in zip(right[row], right[pivot])]
    return right


def horner(coefficients, value):
    total = coefficients[-1] * value + coefficients[-2]
    for entry in coefficients[-3::-1]:
        total = total * value + entry
    return total


def tile_at(step, mine, tiles):
    if tiles == 4:
        high = lax.rem(mine // 2 + 1 - step // 2, 2)
        low = lax.rem(lax.rem(mine, 2) + (step + 1) // 2, 2)
        return 2 * high + low
    return lax.rem(mine + tiles // 2 + step, tiles)


def combine(factors, terms):
    total = terms[0] * factors[0]
    for factor, term in zip(factors[1:], terms[1:]):
        total = total + factor * term
    return total


def tree(terms):
    while len(terms) > 1:
        terms = [sum(terms[at : at + 2]) if at + 1 < len(terms) else terms[at] for at in range(0, len(terms), 2)]
    return terms[0]


def kernel(
    n,
    tiles,
    volts_hbm,
    num_hbm,
    weight_hbm,
    flags_hbm,
    positions_hbm,
    directions_hbm,
    pointing_hbm,
    power_ref,
    gains_ref,
    num_ref,
    weight_ref,
    flags_ref,
    positions_ref,
    directions_ref,
    pointing_ref,
    volts,
    message,
    gathered,
    outbox,
    inbox,
    ordered,
    products,
    phasors,
    ready,
    columns,
    table,
    pointed,
    local_ref,
    dual_ref,
    load_sem,
    cal_send,
    cal_recv,
    fit_send,
    fit_recv,
    out_send,
    out_recv,
    own_sem,
):
    me = lax.axis_index("chan")
    stations = flags_ref.shape[1]
    blocks = stations // LANES
    width = phasors.shape[2]
    samples = volts.shape[1]
    half = samples // 2
    per_device = ready.shape[0] // n
    per_tile = n // tiles
    share = lax.rem(me, blocks)

    loads = [
        pltpu.make_async_copy(source, target, load_sem.at[index])
        for index, (source, target) in enumerate(
            (
                (num_hbm.at[0], num_ref),
                (weight_hbm.at[0], weight_ref),
                (flags_hbm, flags_ref),
                (positions_hbm, positions_ref),
                (directions_hbm, directions_ref),
                (pointing_hbm, pointing_ref),
                (volts_hbm.at[0], volts),
            )
        )
    ]
    for load in loads:
        load.start()

    barrier = pltpu.get_barrier_semaphore()

    @pl.loop(1, n)
    def _(offset):
        pl.semaphore_signal(
            barrier,
            inc=1,
            device_id={"chan": lax.rem(me + offset, n)},
            device_id_type=pl.DeviceIdType.MESH,
        )

    for load in loads[:3]:
        load.wait()
    for block in range(blocks):
        lanes = pl.ds(block * LANES, LANES)
        mask = flags_ref[:, lanes].astype(jnp.float32)
        message[block, 0:4, :] = mask * num_ref[:, lanes]
        for row in range(4):
            message[block, pl.ds(4 + row, 1), :] = mask * weight_ref[pl.ds(row // 2, 1), lanes]
    gathered[me] = message[share]

    pl.semaphore_wait(barrier, n - 1)

    def cal_copy(block, slot, peer, sent, received):
        return pltpu.make_async_remote_copy(
            src_ref=message.at[block],
            dst_ref=gathered.at[slot],
            send_sem=cal_send.at[sent],
            recv_sem=cal_recv.at[received],
            device_id={"chan": peer},
            device_id_type=pl.DeviceIdType.MESH,
        )

    @pl.loop(1, n)
    def _(offset):
        peer = lax.rem(me + offset, n)
        cal_copy(lax.rem(peer, blocks), me, peer, peer, me).start()

    for load in loads[3:6]:
        load.wait()
    for axis in range(2):
        for block in range(blocks):
            lanes = pl.ds(block * LANES, LANES)
            row = jnp.broadcast_to(positions_ref[pl.ds(axis, 1), lanes], (LANES, LANES))
            columns[axis, lanes, :] = row.T

    rest = directions_ref[...]
    table[...] = jnp.zeros_like(table)
    for term in range(3):
        head = rest.astype(jnp.bfloat16).astype(jnp.float32)
        table[pl.ds(8 * term, 2), :] = head
        rest = rest - head
    ratio = 1.0 + 0.15 * (2.0 * (me.astype(jnp.float32) + 0.5) / n)
    entries = directions_ref.shape[1]
    chunk = 32

    @pl.loop(0, tiles)
    def _(tile):
        numbers = lax.broadcasted_iota(jnp.int32, (entries, width), 0)
        chosen = jnp.where(numbers == pointing_ref[tile], 1.0, 0.0).astype(jnp.bfloat16)
        terms = table[...].astype(jnp.bfloat16)
        found = jnp.dot(terms, chosen, preferred_element_type=jnp.float32)
        pointed[tile] = (found[0:8] + found[8:16] + found[16:24]) * ratio

    def make_phasors(step):
        tile = tile_at(step, me // per_tile, tiles)
        east = pointed[tile, 0:1, :]
        north = pointed[tile, 1:2, :]

        @pl.loop(0, stations // chunk)
        def _(part):
            rows = pl.ds(pl.multiple_of(part * chunk, chunk), chunk)
            below = pl.ds(pl.multiple_of(stations + part * chunk, chunk), chunk)
            for piece in range(width // LANES):
                lanes = pl.ds(piece * LANES, LANES)
                cut = slice(piece * LANES, (piece + 1) * LANES)
                turns = columns[0, rows, :] * east[:, cut] + columns[1, rows, :] * north[:, cut]
                turns = turns - ((turns + ROUNDING) - ROUNDING)
                square = turns * turns
                sine = horner(SINE, square) * turns
                cosine = horner(COSINE, square)
                phasors[step, rows, lanes] = (1.0 - sine * sine).astype(jnp.bfloat16)
                phasors[step, below, lanes] = (sine * cosine).astype(jnp.bfloat16)

    make_phasors(0)

    @pl.loop(1, n)
    def _(offset):
        peer = lax.rem(me + offset, n)
        cal_copy(0, peer, peer, peer, peer).wait_recv()

    pairs = n // 2
    basis = [basis_at(2.0 * (n - pair - 0.5) / n - 1.0) for pair in range(pairs)]
    sign = jnp.where(lax.broadcasted_iota(jnp.int32, (8, LANES), 0) < 4, 1.0, -1.0)
    solve_rows = []
    for pair in range(pairs):
        first = gathered[n - 1 - pair]
        second = gathered[pair]
        weight = jnp.concatenate([first[4:8], second[4:8]], axis=0)
        usable = jnp.where(weight > 0.0, 1.0, 0.0)
        damping = 1.0 / (weight + PENALTY)
        target = jnp.concatenate([first[0:4], second[0:4]], axis=0) * damping
        solve_rows.append((usable, PENALTY * damping, target))

    def both(term, value):
        value = value * sign if term % 2 else value
        return value + pltpu.roll(value, 4, 0)

    gram = [[None] * ORDER for _ in range(ORDER)]
    for first in range(ORDER):
        for second in range(first, ORDER):
            terms = [
                (basis[pair][first] * basis[pair][second]) * solve_rows[pair][0]
                for pair in range(pairs)
            ]
            gram[first][second] = both(first + second, tree(terms))
            gram[second][first] = gram[first][second]
        gram[first][first] = gram[first][first] + RIDGE
    inverse = invert_small(gram)
    local_ref[...] = jnp.zeros_like(local_ref)
    dual_ref[...] = jnp.zeros_like(dual_ref)
    nothing = jnp.zeros((8, LANES), jnp.float32)

    def sweep(_, line):
        signed = [entry * sign if term % 2 else entry for term, entry in enumerate(line)]
        numerator = [[] for _ in range(ORDER)]
        for pair in range(pairs):
            values = basis[pair]
            usable, damping, target = solve_rows[pair]
            fitted = tree([signed[0]] + [values[term] * signed[term] for term in range(1, ORDER)])
            dual = dual_ref[pair] + usable * (local_ref[pair] - fitted)
            local = target + damping * (fitted - dual)
            local_ref[pair] = local
            dual_ref[pair] = dual
            summand = usable * (local + dual)
            for term in range(ORDER):
                numerator[term].append(values[term] * summand if term else summand)
        sums = [both(term, tree(terms)) for term, terms in enumerate(numerator)]
        return tuple(
            tree([entry * total for entry, total in zip(inverse[first], sums)])
            for first in range(ORDER)
        )

    line = lax.fori_loop(0, ITERS, sweep, (nothing,) * ORDER)
    line = [entry[0:4] for entry in line]

    def fitted_at(channel):
        return combine(basis_at(2.0 * (channel.astype(jnp.float32) + 0.5) / n - 1.0), line)

    def fit_copy(source, slot, peer, sent, received):
        return pltpu.make_async_remote_copy(
            src_ref=outbox.at[source],
            dst_ref=inbox.at[slot],
            send_sem=fit_send.at[sent],
            recv_sem=fit_recv.at[received],
            device_id={"chan": peer},
            device_id_type=pl.DeviceIdType.MESH,
        )

    for offset in range(1, blocks):
        mate = lax.rem(share + offset, blocks)
        peer = me - share + mate
        outbox[mate] = fitted_at(peer)
        fit_copy(mate, share, peer, mate, share).start()
    inbox[share] = fitted_at(me)

    loads[6].wait()
    row = lax.broadcasted_iota(jnp.int32, (samples, samples), 0)
    col = lax.broadcasted_iota(jnp.int32, (samples, samples), 1)
    origin = jnp.where(row < half, 2 * row, 2 * (row - half) + 1)
    shuffle = jnp.where(col == origin, 1.0, 0.0).astype(jnp.bfloat16)
    for polar in range(2):
        ordered[polar] = jnp.dot(shuffle, volts[polar], preferred_element_type=jnp.float32)

    for offset in range(1, blocks):
        mate = lax.rem(share + offset, blocks)
        fit_copy(mate, mate, me - share + mate, mate, mate).wait_recv()
    for block in range(blocks):
        gains_ref[0, :, pl.ds(block * LANES, LANES)] = inbox[block]

    scale = flags_ref[...].astype(jnp.float32) * stations ** (-0.5)
    strip = 64
    for polar in range(2):
        gain_re = gains_ref[0, pl.ds(2 * polar, 1), :] * scale
        gain_im = gains_ref[0, pl.ds(2 * polar + 1, 1), :] * scale

        @pl.loop(0, samples // strip)
        def _(step):
            rows = pl.ds(pl.multiple_of(step * strip, strip), strip)
            real = ordered[polar, rows, :stations]
            imag = ordered[polar, rows, stations:]
            new_re = (gain_re * real + gain_im * imag).astype(jnp.bfloat16)
            new_im = (gain_re * imag - gain_im * real).astype(jnp.bfloat16)
            upper = pl.ds(pl.multiple_of(2 * polar * samples + step * strip, strip), strip)
            lower = pl.ds(pl.multiple_of((2 * polar + 1) * samples + step * strip, strip), strip)
            products[upper, :stations] = new_re
            products[upper, stations:] = new_im
            products[lower, :stations] = new_im
            products[lower, stations:] = -new_re

    def out_copy(owner, source, sent, received):
        rows = pl.ds(pl.multiple_of(owner * per_device, per_device), per_device)
        return pltpu.make_async_remote_copy(
            src_ref=ready.at[rows, :],
            dst_ref=power_ref.at[source],
            send_sem=out_send.at[sent],
            recv_sem=out_recv.at[received],
            device_id={"chan": owner},
            device_id_type=pl.DeviceIdType.MESH,
        )

    def own_copy():
        rows = pl.ds(pl.multiple_of(me * per_device, per_device), per_device)
        return pltpu.make_async_copy(ready.at[rows, :], power_ref.at[me], own_sem)

    @pl.loop(0, tiles)
    def _(step):
        @pl.when(step >= 1)
        def _():
            make_phasors(step)

        tile = tile_at(step, me // per_tile, tiles)
        beams = jnp.dot(products[...], phasors[step], preferred_element_type=jnp.float32)
        total = beams[:samples] * beams[:samples]
        for part in range(1, 4):
            piece = beams[part * samples : (part + 1) * samples]
            total = total + piece * piece
        mean = (total[:half] + total[half:]) * 0.5
        rows = pl.ds(pl.multiple_of(tile * width, width), width)
        ready[rows, :] = mean.T.astype(jnp.bfloat16)

        @pl.loop(0, per_tile)
        def _(index):
            owner = tile * per_tile + index

            @pl.when(owner != me)
            def _():
                out_copy(owner, me, owner, me).start()

            @pl.when(owner == me)
            def _():
                own_copy().start()

    own_copy().wait()
    for offset in range(1, blocks):
        mate = lax.rem(share + offset, blocks)
        fit_copy(mate, share, me - share + mate, mate, share).wait_send()

    @pl.loop(1, n)
    def _(offset):
        peer = lax.rem(me + offset, n)
        cal_copy(lax.rem(peer, blocks), me, peer, peer, me).wait_send()
        out_copy(peer, me, peer, me).wait_send()
        out_copy(peer, peer, peer, peer).wait_recv()


def body(voltages, cal_num, cal_weight, flags, positions, directions, pointing):
    n = lax.axis_size("chan")
    count, polars, samples, depth = voltages.shape
    stations = flags.shape[1]
    blocks = stations // LANES
    assert count == 1 and polars == 2 and n % blocks == 0 and n % 2 == 0
    beams = pointing.shape[0]
    tiles = 4
    width = beams // tiles
    half = samples // 2
    entries = directions.shape[1]
    vmem = pl.BlockSpec(memory_space=pltpu.VMEM)
    hbm = pl.BlockSpec(memory_space=pltpu.HBM)
    f32 = jnp.float32
    power, gains = pl.pallas_call(
        functools.partial(kernel, n, tiles),
        out_shape=(
            pltpu.VMEM((n, beams // n, half), jnp.bfloat16),
            jax.ShapeDtypeStruct(cal_num.shape, f32),
        ),
        in_specs=[hbm] * 7,
        out_specs=(vmem, vmem),
        scratch_shapes=[
            pltpu.VMEM(cal_num.shape[1:], f32),
            pltpu.VMEM(cal_weight.shape[1:], f32),
            pltpu.VMEM(flags.shape, jnp.int32),
            pltpu.VMEM(positions.shape, f32),
            pltpu.VMEM(directions.shape, f32),
            pltpu.VMEM((tiles, 1, width), jnp.int32),
            pltpu.VMEM((polars, samples, depth), jnp.bfloat16),
            pltpu.VMEM((blocks, 8, LANES), f32),
            pltpu.VMEM((n, 8, LANES), f32),
            pltpu.VMEM((blocks, 4, LANES), f32),
            pltpu.VMEM((blocks, 4, LANES), f32),
            pltpu.VMEM((polars, samples, depth), f32),
            pltpu.VMEM((4 * samples, depth), jnp.bfloat16),
            pltpu.VMEM((tiles, depth, width), jnp.bfloat16),
            pltpu.VMEM((beams, half), jnp.bfloat16),
            pltpu.VMEM((2, stations, LANES), f32),
            pltpu.VMEM((32, entries), f32),
            pltpu.VMEM((tiles, 8, width), f32),
            pltpu.VMEM((n // 2, 8, LANES), f32),
            pltpu.VMEM((n // 2, 8, LANES), f32),
            pltpu.SemaphoreType.DMA((7,)),
            pltpu.SemaphoreType.DMA((n,)),
            pltpu.SemaphoreType.DMA((n,)),
            pltpu.SemaphoreType.DMA((blocks,)),
            pltpu.SemaphoreType.DMA((blocks,)),
            pltpu.SemaphoreType.DMA((n,)),
            pltpu.SemaphoreType.DMA((n,)),
            pltpu.SemaphoreType.DMA,
        ],
        compiler_params=pltpu.CompilerParams(
            collective_id=0, has_side_effects=True, vmem_limit_bytes=40 * 2**20
        ),
    )(
        *(
            pltpu.with_memory_space_constraint(operand, pltpu.HBM)
            for operand in (
                voltages,
                cal_num,
                cal_weight,
                flags,
                positions,
                directions,
                pointing.reshape(tiles, 1, width),
            )
        )
    )
    return jnp.transpose(power, (1, 0, 2)), gains


def solution(mesh):
    return jax.shard_map(
        body,
        mesh=mesh,
        in_specs=(
            P(("group", "chan"), None, None, None),
            P(("group", "chan"), None, None),
            P(("group", "chan"), None, None),
            P(("group", "chan"), None),
            P(),
            P(),
            P("group"),
        ),
        out_specs=(P(("group", "chan"), None, None), P(("group", "chan"), None, None)),
        check_vma=False,
    )
```
